256 devices in a mesh: dp: 16 (over x_lo, y, core), space: 16 (over z, x_hi).
Axes of the slice: x: 4 (x_hi: 2, x_lo: 2; x = x_hi * 2 + x_lo), y: 4, z: 8, core: 2. Of those that a mesh axis runs over, the one named last changes fastest.
Arguments:
- features: bfloat16 [16, 32, 8, 8, 256], P('dp', 'space'), may hold values from -6 to 6
- weight_one: bfloat16 [27, 256, 256], P(None, 'dp'), may hold values from -0.078125 to 0.078125
- weight_two: bfloat16 [27, 256, 256], P(None, 'dp'), may hold values from -0.078125 to 0.078125
- cotangent: bfloat16 [16, 32, 8, 8, 256], P('dp', 'space'), may hold values from -6 to 6
Outputs:
- output: bfloat16 [16, 32, 8, 8, 256], P('dp', 'space')
- grad_input: bfloat16 [16, 32, 8, 8, 256], P('dp', 'space')
- grad_one: float32 [27, 256, 256], P(None, 'dp')
- grad_two: float32 [27, 256, 256], P(None, 'dp')
The draws below stay inside these ranges and needn't reach their ends.
All inputs are finite; a program needn't handle non-finite values.
Results may differ from the reference program's by a relative error of at most 0.003.
Values may be sent and summed in bfloat16 or wider, within the bound.
A program may use at most 128 MiB of HBM per device.

```python
import jax
import jax.numpy as jnp
from jax import lax

C = 256
NY = 8
NZ = 8
SAMPLES = 16
NX = 32


def levels(own_key, dims, cuts, low, high):
    loudness, own = 1.0, jax.random.fold_in(own_key, 6)
    for axis_at, blocks in cuts:
        heights = jnp.exp(jax.random.uniform(jax.random.fold_in(own, axis_at), (blocks,), jnp.float32, low / len(cuts), high / len(cuts)))
        loudness = loudness * jnp.repeat(heights, dims[axis_at] // blocks).reshape([-1 if axis == axis_at else 1 for axis in range(len(dims))])
    return loudness


def gaussian(rng, extent, deviation, reach, cuts=(), dtype=jnp.bfloat16):
    drawn = jax.random.normal(rng, extent, jnp.float32) * deviation
    if len(cuts) > 0:
        drawn = levels(rng, extent, cuts, -0.22, 0.18) * drawn
    return jnp.clip(drawn, min=-reach, max=reach).astype(dtype)


def setup_inputs(seed: int = 0) -> dict:
    streams_of = jax.random.split(jax.random.key(seed), 5)
    features = gaussian(streams_of[0], (SAMPLES, NX, NY, NZ, C), 1.0, 6.0, ((0, 16), (1, 16)))
    weight_one = gaussian(streams_of[1], (27, C, C), (27 * C) ** -0.5, 0.078125, ((1, 16),))
    weight_two = gaussian(streams_of[2], (27, C, C), (27 * C) ** -0.5, 0.078125, ((1, 16),))
    cotangent = gaussian(streams_of[3], (SAMPLES, NX, NY, NZ, C), 1.0, 6.0, ((0, 16), (1, 16)))
    return {"features": features, "weight_one": weight_one, "weight_two": weight_two, "cotangent": cotangent}


def stencil_taps(padded, plane):
    depth_x = padded.shape[1] - 2
    depth_y = padded.shape[2] - 2
    depth_z = padded.shape[3] - 2
    chans = padded.shape[4]
    pieces = [padded[:, plane:plane + depth_x, j:j + depth_y, k:k + depth_z, :] for j in range(3) for k in range(3)]
    return jnp.stack(pieces, axis=-2).reshape(-1, 9 * chans)


def convolve(padded, kernel):
    chans = padded.shape[4]
    total = jnp.zeros((1,), jnp.float32)
    for plane in range(3):
        block = kernel[9 * plane:9 * plane + 9].reshape(9 * chans, -1)
        total = total + jnp.dot(stencil_taps(padded, plane), block, preferred_element_type=jnp.float32)
    return total


def weight_terms(padded, grad_out):
    chans = padded.shape[4]
    flat = grad_out.reshape(-1, grad_out.shape[-1])
    parts = [lax.dot_general(stencil_taps(padded, plane), flat, (((0,), (0,)), ((), ())), preferred_element_type=jnp.float32) for plane in range(3)]
    return jnp.concatenate(parts, axis=0).reshape(27, chans, flat.shape[1])


def flip_kernel(kernel):
    return jnp.flip(kernel, 0).transpose(0, 2, 1)


def pad_grid(volume):
    return jnp.pad(volume, ((0, 0), (1, 1), (1, 1), (1, 1), (0, 0)))


def reference(features, weight_one, weight_two, cotangent):
    back_one = flip_kernel(weight_one)
    back_two = flip_kernel(weight_two)

    def one_sample(pair):
        sample, grad_out = pair
        sample = sample[None]
        grad_out = grad_out[None]
        x_pad = pad_grid(sample)
        pre = convolve(x_pad, weight_one)
        activated = jax.nn.silu(pre).astype(jnp.bfloat16).reshape(sample.shape)
        act_pad = pad_grid(activated)
        second = convolve(act_pad, weight_two)
        output = (sample.reshape(-1, C).astype(jnp.float32) + second).astype(jnp.bfloat16)
        grad_act = convolve(pad_grid(grad_out), back_two)
        sig = jax.nn.sigmoid(pre)
        grad_pre = (grad_act * sig * (1.0 + pre * (1.0 - sig))).astype(jnp.bfloat16).reshape(sample.shape)
        grad_input = (grad_out.reshape(-1, C).astype(jnp.float32) + convolve(pad_grid(grad_pre), back_one)).astype(jnp.bfloat16)
        grad_two = weight_terms(act_pad, grad_out)
        grad_one = weight_terms(x_pad, grad_pre)
        return output.reshape(sample.shape[1:]), grad_input.reshape(sample.shape[1:]), grad_one, grad_two

    outputs, grads_in, grads_one, grads_two = lax.map(one_sample, (features, cotangent))
    factor = float(SAMPLES * NX * NY * NZ) ** -0.5
    return outputs, grads_in, jnp.sum(grads_one, axis=0) * factor, jnp.sum(grads_two, axis=0) * factor
```

```python
import functools

import jax
import jax.numpy as jnp
from jax import lax
from jax.experimental import pallas as pl
from jax.experimental.pallas import tpu as pltpu
from jax.sharding import PartitionSpec as P

MESH = pl.DeviceIdType.MESH
F32 = jnp.float32
BF16 = jnp.bfloat16
C = 256
TAPS = 27
ROWS = TAPS * 16


def dot(a, b, dims=((1,), (0,))):
    return lax.dot_general(a, b, (dims, ((), ())), preferred_element_type=F32)


def lanes():
    return lax.broadcasted_iota(jnp.int32, (16, 128), 1)


def lower():
    return lanes() % 128 < 64


def half_turn(v):
    return pltpu.roll(v, 64, 1)


def inside(j, k, sign):
    lane = lanes()
    y = (lane // 8) % 8 + sign * (j - 1)
    z = lane % 8 + sign * (k - 1)
    return (y >= 0) & (y < 8) & (z >= 0) & (z < 8)


def shifted(v, j, k, sign):
    delta = sign * (8 * (j - 1) + (k - 1))
    if delta == 0:
        return v
    parts = v.shape[0] // 16
    keep = inside(j, k, sign)
    if parts > 1:
        keep = jnp.concatenate([keep] * parts, axis=0)
    return jnp.where(keep, pltpu.roll(v, (-delta) % 128, 1), 0.0)


def regroup(w_ref, z_ref):
    group = lanes() // 16
    for q in range(4):
        for h in range(2):
            tiles = []
            for i in range(8):
                tap = 8 * q + i
                if tap < TAPS:
                    tiles.append(w_ref[16 * tap : 16 * tap + 16, 128 * h : 128 * h + 128].astype(F32))
                else:
                    tiles.append(jnp.zeros((16, 128), F32))
            for bit in (1, 2, 4):
                low = (group & bit) == 0
                for i in range(8):
                    if i & bit:
                        continue
                    a, b = tiles[i], tiles[i + bit]
                    tiles[i] = jnp.where(low, a, pltpu.roll(b, 16 * bit, 1))
                    tiles[i + bit] = jnp.where(low, pltpu.roll(a, 128 - 16 * bit, 1), b)
            for i in range(8):
                z_ref[8 * h + i, :, 128 * q : 128 * q + 128] = tiles[i].astype(BF16)


def gather_taps(y_ref, p_ref, hm_ref, hp_ref, tensor, chip, sign):
    lo = lower()
    lefts = []
    for half in range(2):
        at = slice(128 * half, 128 * half + 128)
        total = None
        for j in range(3):
            for k in range(3):
                rows = [16 * (9 * i + 3 * j + k) for i in range(3)]
                first, mid, last = [y_ref[r : r + 16, at] for r in rows]
                if sign < 0:
                    first, last = last, first
                inner = jnp.where(lo, first, last)
                outer = jnp.where(lo, last, first)
                term = shifted(jnp.concatenate([mid, inner, outer], axis=0), j, k, sign)
                total = term if total is None else total + term
        p_ref[tensor, chip, :, at] = total[:16] + half_turn(total[16:32])
        lefts.append(total[32:])
    hm_ref[tensor, chip] = jnp.where(lo, lefts[0], half_turn(lefts[1]))
    hp_ref[tensor, chip] = jnp.where(lo, half_turn(lefts[0]), lefts[1])


def spread_halo(hp, hm, first, final):
    lo = lower()
    hp = jnp.where(first, 0.0, hp)
    hm = jnp.where(final, 0.0, hm)
    return [jnp.where(lo, hp, half_turn(hm)), jnp.where(lo, half_turn(hp), hm)]


def edge_planes(v):
    lo = lower()
    a, b = v[:, :128], v[:, 128:]
    return jnp.where(lo, a, half_turn(b)), jnp.where(lo, half_turn(a), b)


def scatter_taps(v, halos, im_ref, chip):
    lo = lower()
    for half in range(2):
        at = slice(128 * half, 128 * half + 128)
        own = v[:, at]
        turned = half_turn(own)
        stack = jnp.concatenate(
            [jnp.where(lo, halos[half], turned), own, jnp.where(lo, turned, halos[half])], axis=0
        )
        for j in range(3):
            for k in range(3):
                term = shifted(stack, j, k, 1).astype(BF16)
                for i in range(3):
                    row = 16 * (9 * i + 3 * j + k)
                    im_ref[chip, row : row + 16, at] = term[16 * i : 16 * i + 16]


def kernel(
    factor,
    x_ref, g_ref, w1_ref, w2_ref,
    out_ref, gin_ref, one_ref, two_ref,
    ga, gb, z1, z2, r1, r2, f1, f2, y_ref, p_ref, hm, hp, rhm, rhp,
    xm, xp, rxm, rxp, am, ap, ram, rap, imx, ima, gsum, gb16, rr, full, oc, oall,
    w_send, w_recv, a_send, a_recv, s_send, s_recv, b_send, b_recv, t_send, t_recv,
    n_send, n_recv, r_send, r_recv, f_send, f_recv, o_send, o_recv,
):
    d = lax.axis_index("dp")
    s = lax.axis_index("space")
    m = d // 2
    e = d - 2 * m
    above = lax.rem(s + 1, 16)
    below = lax.rem(s + 15, 16)
    first, final = s == 0, s == 15
    sibling = 2 * m + 1 - e
    core_at = pl.ds(pl.multiple_of(e * 128, 128), 128)
    core_other = pl.ds(pl.multiple_of((1 - e) * 128, 128), 128)
    own_rows = pl.ds(pl.multiple_of(d * 16, 16), 16)

    def rows_of(index, count):
        return pl.ds(pl.multiple_of(index * count, count), count)

    def remote(src, dst, send, recv, dp, space):
        return pltpu.make_async_remote_copy(
            src_ref=src, dst_ref=dst, send_sem=send, recv_sem=recv, device_id=(dp, space), device_id_type=MESH
        )

    def each(count, body, start=0):
        def step(i, carry):
            body(i)
            return carry

        lax.fori_loop(start, count, step, 0)

    barrier = pltpu.get_barrier_semaphore()

    def greet(r):
        pl.semaphore_signal(barrier, inc=1, device_id=(lax.rem(d + r, 16), s), device_id_type=MESH)
        pl.semaphore_signal(barrier, inc=1, device_id=(d, lax.rem(s + r, 16)), device_id_type=MESH)

    each(16, greet, 1)

    ga[m, 0, :, core_at] = x_ref[...].astype(F32).T.astype(BF16)
    ga[m, 1, :, core_at] = g_ref[...].astype(F32).T.astype(BF16)
    regroup(w1_ref, z1)
    regroup(w2_ref, z2)
    gb16[:, ROWS:, :] = jnp.zeros((2, 80, C), BF16)
    pl.semaphore_wait(barrier, 30)

    def send_slices(which, z, r):
        def body(step):
            to = lax.rem(d + step, 16)
            remote(z.at[to], r.at[own_rows], w_send.at[which, to], w_recv.at[which, d], to, s).start()

        each(16, body, 1)
        r[own_rows] = z[d]

    def wait_slices(which, z, r):
        def body(step):
            at = lax.rem(d + 16 - step, 16)
            copy = remote(z.at[at], r.at[rows_of(at, 16)], w_send.at[which, at], w_recv.at[which, at], at, s)
            copy.wait_recv()
            copy.wait_send()

        each(16, body, 1)

    def block_a(chip, where):
        return ga.at[chip, :, :, where]

    def across_a(step, chip):
        to = lax.rem(m + step, 8)
        return remote(block_a(chip, core_at), block_a(chip, core_at), a_send.at[step], a_recv.at[chip], 2 * to + e, s)

    def beside_a(chip, where):
        return remote(block_a(chip, where), block_a(chip, where), s_send.at[chip], s_recv.at[chip], sibling, s)

    send_slices(0, z1, r1)
    beside_a(m, core_at).start()
    each(8, lambda step: across_a(step, m).start(), 1)
    send_slices(1, z2, r2)
    wait_slices(0, z1, r1)
    f1[...] = r1[...].astype(F32).T.astype(BF16)

    def phase_one(step):
        @pl.when(step < 8)
        def _():
            chip = lax.rem(m + 8 - step, 8)
            across_a(step, chip).wait_recv()
            beside_a(chip, core_at).start()

        chip = lax.rem(m + 9 - step, 8)
        beside_a(chip, core_other).wait_recv()
        y_ref[...] = dot(f1[:ROWS], ga[chip, 0])
        gather_taps(y_ref, p_ref, hm.at[0], hp.at[0], 0, chip, 1)
        y_ref[...] = dot(w2_ref[...], ga[chip, 1])
        gather_taps(y_ref, p_ref, hm.at[0], hp.at[0], 1, chip, -1)

    each(9, phase_one, 1)

    def near(index, src, dst, to):
        return remote(src, dst, n_send.at[index], n_recv.at[index], d, to)

    near(0, hm.at[0], rhm.at[0], below).start()
    near(1, hp.at[0], rhp.at[0], above).start()

    def x_edges(chip):
        v = ga[chip, 0, own_rows, :].astype(F32)
        lowest, highest = edge_planes(v)
        xm[chip] = lowest.astype(BF16)
        xp[chip] = highest.astype(BF16)

    each(8, x_edges)
    near(2, xm, rxm, below).start()
    near(3, xp, rxp, above).start()

    near(0, hm.at[0], rhm.at[0], below).wait_recv()
    near(1, hp.at[0], rhp.at[0], above).wait_recv()

    def middle(chip):
        halo = [spread_halo(rhp[0, t, chip], rhm[0, t, chip], first, final) for t in range(2)]
        pre = p_ref[0, chip] + jnp.concatenate(halo[0], axis=1)
        grad = p_ref[1, chip] + jnp.concatenate(halo[1], axis=1)
        sig = jax.nn.sigmoid(pre)
        act = (pre * sig).astype(BF16)
        gb[0, chip, own_rows, :] = act
        gb[1, chip, own_rows, :] = (grad * sig * (1.0 + pre * (1.0 - sig))).astype(BF16)
        lowest, highest = edge_planes(act.astype(F32))
        am[chip] = lowest.astype(BF16)
        ap[chip] = highest.astype(BF16)

    each(8, middle)

    def block_b(tensor, owner):
        return gb.at[tensor, :, rows_of(owner, 16), :]

    def across_b(tensor, step, owner):
        to = 2 * lax.rem(m + step, 8) + e
        return remote(
            block_b(tensor, owner), block_b(tensor, owner),
            b_send.at[tensor, step], b_recv.at[tensor, owner // 2], to, s,
        )

    def beside_b(tensor, owner):
        return remote(
            block_b(tensor, owner), block_b(tensor, owner),
            t_send.at[tensor, owner // 2], t_recv.at[tensor, owner // 2], sibling, s,
        )

    near(4, am, ram, below).start()
    near(5, ap, rap, above).start()
    for tensor in (1, 0):
        beside_b(tensor, d).start()
        each(8, lambda step: across_b(tensor, step, d).start(), 1)

    near(2, xm, rxm, below).wait_recv()
    near(3, xp, rxp, above).wait_recv()

    def taps_x(chip):
        halos = spread_halo(rxp[chip].astype(F32), rxm[chip].astype(F32), first, final)
        scatter_taps(ga[chip, 0, own_rows, :].astype(F32), halos, imx, chip)

    each(8, taps_x)

    near(4, am, ram, below).wait_recv()
    near(5, ap, rap, above).wait_recv()

    def taps_a(chip):
        halos = spread_halo(rap[chip].astype(F32), ram[chip].astype(F32), first, final)
        scatter_taps(gb[0, chip, own_rows, :].astype(F32), halos, ima, chip)

    each(8, taps_a)

    def reduce_copy(which, to, source):
        return remote(
            gb16.at[which, rows_of(to, 32)], rr.at[which, source],
            r_send.at[which, to], r_recv.at[which, source], d, to,
        )

    def send_partial(which, im, operand):
        gsum[...] = dot(im[0], operand(0), ((1,), (1,)))

        def add(chip):
            gsum[...] += dot(im[chip], operand(chip), ((1,), (1,)))

        each(8, add, 1)
        gb16[which, :ROWS] = gsum[...].astype(BF16)
        each(16, lambda step: reduce_copy(which, lax.rem(s + step, 16), s).start(), 1)
        rr[which, s] = gb16[which, rows_of(s, 32)]

    def spread_copy(which, to, owner):
        block = full.at[which, rows_of(owner, 32)]
        return remote(block, block, f_send.at[which, to], f_recv.at[which, owner], d, to)

    def reduce(which):
        def body(step):
            source = lax.rem(s + 16 - step, 16)
            reduce_copy(which, source, source).wait_recv()

        each(16, body, 1)
        total = rr[which, 0].astype(F32)
        for source in range(1, 16):
            total += rr[which, source].astype(F32)
        full[which, rows_of(s, 32)] = total * factor
        each(16, lambda step: spread_copy(which, lax.rem(s + step, 16), s).start(), 1)

    send_partial(1, ima, lambda chip: ga[chip, 1])

    def arrive_b(tensor):
        def forward(step):
            owner = 2 * lax.rem(m + 8 - step, 8) + e
            across_b(tensor, step, owner).wait_recv()
            beside_b(tensor, owner).start()

        each(8, forward, 1)
        each(8, lambda chip: beside_b(tensor, 2 * chip + 1 - e).wait_recv())

    arrive_b(1)
    send_partial(0, imx, lambda chip: gb[1, chip])
    arrive_b(0)
    wait_slices(1, z2, r2)
    f2[...] = r2[...].astype(F32).T.astype(BF16)
    reduce(1)

    def phase_two(chip):
        y_ref[...] = dot(f2[:ROWS], gb[0, chip])
        gather_taps(y_ref, p_ref, hm.at[1], hp.at[1], 0, chip, 1)
        y_ref[...] = dot(w1_ref[...], gb[1, chip])
        gather_taps(y_ref, p_ref, hm.at[1], hp.at[1], 1, chip, -1)

    each(8, phase_two)
    near(6, hm.at[1], rhm.at[1], below).start()
    near(7, hp.at[1], rhp.at[1], above).start()
    reduce(0)
    near(6, hm.at[1], rhm.at[1], below).wait_recv()
    near(7, hp.at[1], rhp.at[1], above).wait_recv()

    def finish(chip):
        for t in range(2):
            halo = spread_halo(rhp[1, t, chip], rhm[1, t, chip], first, final)
            total = p_ref[t, chip] + jnp.concatenate(halo, axis=1)
            total = (ga[chip, t, own_rows, :].astype(F32) + total).astype(BF16)
            oc[t, 2 * chip] = total[:, :128]
            oc[t, 2 * chip + 1] = total[:, 128:]

    each(8, finish)

    def home(t, to, source):
        return remote(
            oc.at[t, to], oall.at[t, rows_of(source, 16)], o_send.at[t, to], o_recv.at[t, source], to, s
        )

    def send_home(step):
        for t in range(2):
            home(t, lax.rem(d + step, 16), d).start()

    each(16, send_home, 1)
    for t in range(2):
        oall[t, own_rows] = oc[t, d]

    def wait_home(step):
        for t in range(2):
            source = lax.rem(d + 16 - step, 16)
            home(t, source, source).wait_recv()

    each(16, wait_home, 1)
    out_ref[...] = oall[0].astype(F32).T.astype(BF16)
    gin_ref[...] = oall[1].astype(F32).T.astype(BF16)

    def wait_spread(step):
        for which in range(2):
            owner = lax.rem(s + 16 - step, 16)
            spread_copy(which, owner, owner).wait_recv()

    each(16, wait_spread, 1)
    one_ref[...] = full[0, :ROWS]
    two_ref[...] = full[1, :ROWS]

    def wait_far(step):
        to = lax.rem(s + step, 16)
        for which in range(2):
            reduce_copy(which, to, s).wait_send()
            spread_copy(which, to, s).wait_send()
            home(which, lax.rem(d + step, 16), d).wait_send()

    each(16, wait_far, 1)

    def wait_across(step):
        across_a(step, m).wait_send()
        for tensor in range(2):
            across_b(tensor, step, d).wait_send()

    each(8, wait_across, 1)

    def wait_beside(chip):
        beside_a(chip, core_at).wait_send()
        for tensor in range(2):
            beside_b(tensor, 2 * chip + e).wait_send()

    each(8, wait_beside)
    near(0, hm.at[0], rhm.at[0], below).wait_send()
    near(1, hp.at[0], rhp.at[0], above).wait_send()
    near(2, xm, rxm, below).wait_send()
    near(3, xp, rxp, above).wait_send()
    near(4, am, ram, below).wait_send()
    near(5, ap, rap, above).wait_send()
    near(6, hm.at[1], rhm.at[1], below).wait_send()
    near(7, hp.at[1], rhp.at[1], above).wait_send()


def shards(features, weight_one, weight_two, cotangent):
    shape = features.shape
    count = shape[0] * lax.axis_size("dp") * shape[1] * lax.axis_size("space") * shape[2] * shape[3]
    factor = float(count) ** (-0.5)
    vmem = pl.BlockSpec(memory_space=pltpu.VMEM)
    dma = pltpu.SemaphoreType.DMA
    halo = lambda dtype, *lead: pltpu.VMEM((*lead, 8, 16, 128), dtype)
    out, gin, one, two = pl.pallas_call(
        functools.partial(kernel, factor),
        out_shape=[
            jax.ShapeDtypeStruct((128, C), BF16),
            jax.ShapeDtypeStruct((128, C), BF16),
            jax.ShapeDtypeStruct((ROWS, C), F32),
            jax.ShapeDtypeStruct((ROWS, C), F32),
        ],
        in_specs=[vmem] * 4,
        out_specs=[vmem] * 4,
        scratch_shapes=[
            pltpu.VMEM((8, 2, C, C), BF16),
            pltpu.VMEM((2, 8, C, C), BF16),
            pltpu.VMEM((16, 16, 512), BF16),
            pltpu.VMEM((16, 16, 512), BF16),
            pltpu.VMEM((C, 512), BF16),
            pltpu.VMEM((C, 512), BF16),
            pltpu.VMEM((512, C), BF16),
            pltpu.VMEM((512, C), BF16),
            pltpu.VMEM((ROWS, C), F32),
            pltpu.VMEM((2, 8, 16, C), F32),
            halo(F32, 2, 2), halo(F32, 2, 2), halo(F32, 2, 2), halo(F32, 2, 2),
            halo(BF16), halo(BF16), halo(BF16), halo(BF16),
            halo(BF16), halo(BF16), halo(BF16), halo(BF16),
            pltpu.VMEM((8, ROWS, C), BF16),
            pltpu.VMEM((8, ROWS, C), BF16),
            pltpu.VMEM((ROWS, C), F32),
            pltpu.VMEM((2, 512, C), BF16),
            pltpu.VMEM((2, 16, 32, C), BF16),
            pltpu.VMEM((2, 512, C), F32),
            pltpu.VMEM((2, 16, 16, 128), BF16),
            pltpu.VMEM((2, C, 128), BF16),
            dma((2, 16)), dma((2, 16)),
            dma((8,)), dma((8,)), dma((8,)), dma((8,)),
            dma((2, 8)), dma((2, 8)), dma((2, 8)), dma((2, 8)),
            dma((8,)), dma((8,)),
            dma((2, 16)), dma((2, 16)), dma((2, 16)), dma((2, 16)), dma((2, 16)), dma((2, 16)),
        ],
        compiler_params=pltpu.CompilerParams(
            collective_id=0, has_side_effects=True, vmem_limit_bytes=40 * 2**20
        ),
    )(
        features.reshape(128, C), cotangent.reshape(128, C),
        weight_one.reshape(ROWS, C), weight_two.reshape(ROWS, C),
    )
    return out.reshape(shape), gin.reshape(shape), one.reshape(TAPS, 16, C), two.reshape(TAPS, 16, C)


def solution(mesh):
    in_specs = (
        P("dp", "space", None, None, None),
        P(None, "dp", None),
        P(None, "dp", None),
        P("dp", "space", None, None, None),
    )
    out_specs = (
        P("dp", "space", None, None, None),
        P("dp", "space", None, None, None),
        P(None, "dp", None),
        P(None, "dp", None),
    )
    return jax.shard_map(shards, mesh=mesh, in_specs=in_specs, out_specs=out_specs, check_vma=False)
```

```python
import functools

import jax
import jax.numpy as jnp
from jax import lax
from jax.experimental import pallas as pl
from jax.experimental.pallas import tpu as pltpu
from jax.sharding import PartitionSpec as P

MESH = pl.DeviceIdType.MESH
F32 = jnp.float32
BF16 = jnp.bfloat16
C = 256
TAPS = 27
ROWS = TAPS * 16
TILES = 2 * TAPS
SHARE = -(-TILES // 8)


def dot(a, b, dims=((1,), (0,))):
    return lax.dot_general(a, b, (dims, ((), ())), preferred_element_type=F32)


def lanes():
    return lax.broadcasted_iota(jnp.int32, (16, 128), 1)


def lower(rows=16):
    return lax.broadcasted_iota(jnp.int32, (rows, 128), 1) < 64


def half_turn(v):
    return pltpu.roll(v, 64, 1)


def inside(j, k, sign):
    lane = lanes()
    y = (lane // 8) % 8 + sign * (j - 1)
    z = lane % 8 + sign * (k - 1)
    return (y >= 0) & (y < 8) & (z >= 0) & (z < 8)


def shifted(v, j, k, sign):
    delta = sign * (8 * (j - 1) + (k - 1))
    if delta == 0:
        return v
    parts = v.shape[0] // 16
    keep = inside(j, k, sign)
    if parts > 1:
        keep = jnp.concatenate([keep] * parts, axis=0)
    return jnp.where(keep, pltpu.roll(v, (-delta) % 128, 1), 0.0)


def regroup(w_ref, z_ref):
    group = lanes() // 16
    for q in range(4):
        for h in range(2):
            tiles = []
            for i in range(8):
                tap = 8 * q + i
                if tap < TAPS:
                    tiles.append(w_ref[16 * tap : 16 * tap + 16, 128 * h : 128 * h + 128].astype(F32))
                else:
                    tiles.append(jnp.zeros((16, 128), F32))
            for bit in (1, 2, 4):
                low = (group & bit) == 0
                for i in range(8):
                    if i & bit:
                        continue
                    a, b = tiles[i], tiles[i + bit]
                    tiles[i] = jnp.where(low, a, pltpu.roll(b, 16 * bit, 1))
                    tiles[i + bit] = jnp.where(low, pltpu.roll(a, 128 - 16 * bit, 1), b)
            for i in range(8):
                z_ref[8 * h + i, :, 128 * q : 128 * q + 128] = tiles[i].astype(BF16)


def gather_taps(y_ref, p_ref, hm_ref, hp_ref, sign):
    lo = lower()
    lefts = []
    for half in range(2):
        at = slice(128 * half, 128 * half + 128)
        total = None
        for j in range(3):
            for k in range(3):
                rows = [16 * (9 * i + 3 * j + k) for i in range(3)]
                first, mid, last = [y_ref[r : r + 16, at] for r in rows]
                if sign < 0:
                    first, last = last, first
                inner = jnp.where(lo, first, last)
                outer = jnp.where(lo, last, first)
                term = shifted(jnp.concatenate([mid, inner, outer], axis=0), j, k, sign)
                total = term if total is None else total + term
        p_ref[:, at] = total[:16] + half_turn(total[16:32])
        lefts.append(total[32:])
    hm_ref[...] = jnp.where(lo, lefts[0], half_turn(lefts[1]))
    hp_ref[...] = jnp.where(lo, half_turn(lefts[0]), lefts[1])


def spread_halo(hp, hm, first, final):
    lo = lower(hp.shape[0])
    hp = jnp.where(first, 0.0, hp.astype(F32))
    hm = jnp.where(final, 0.0, hm.astype(F32))
    return [jnp.where(lo, hp, half_turn(hm)), jnp.where(lo, half_turn(hp), hm)]


def edge_planes(v):
    lo = lower(v.shape[0])
    a, b = v[:, :128], v[:, 128:]
    return jnp.where(lo, a, half_turn(b)), jnp.where(lo, half_turn(a), b)


def scatter_taps(v, halos, im_ref):
    lo = lower()
    for half in range(2):
        at = slice(128 * half, 128 * half + 128)
        own = v[:, at]
        turned = half_turn(own)
        stack = jnp.concatenate(
            [jnp.where(lo, halos[half], turned), own, jnp.where(lo, turned, halos[half])], axis=0
        )
        for j in range(3):
            for k in range(3):
                term = shifted(stack, j, k, 1).astype(BF16)
                for i in range(3):
                    row = 16 * (9 * i + 3 * j + k)
                    im_ref[row : row + 16, at] = term[16 * i : 16 * i + 16]


def kernel(
    factor,
    x_hbm, g_hbm, w1_hbm, w2_hbm,
    out_ref, gin_ref, one_ref, two_ref,
    x_ref, g_ref, w1, w2,
    ga, gb, z1, z2, r1, r2, f1, f2, y_ref, p_ref, hm, hp, rhm, rhp,
    xm, xp, rxm, rxp, am, ap, ram, rap, imx, ima, gsum, gout, gin2, mine, sent, rr, part, other, full, oc, oall,
    in_sem, w_send, w_recv, v_send, v_recv, a_send, a_recv,
    h_send, h_recv, n_send, n_recv, c_send, c_recv, r_send, r_recv, x_send, x_recv, f_send, f_recv, o_send, o_recv,
):
    d = lax.axis_index("dp")
    s = lax.axis_index("space")
    m, e = d // 2, d % 2
    xl, y = m // 4, m % 4
    z, xh = s // 2, s % 2
    above = lax.rem(s + 1, 16)
    below = lax.rem(s + 15, 16)
    first, final = s == 0, s == 15
    sibling = 2 * m + 1 - e
    up, down, far = [lax.rem(y + step, 4) for step in (1, 3, 2)]
    side = (1 - xl) * 4
    U, D, O, X = xl * 4 + up, xl * 4 + down, xl * 4 + far, side + y
    XU, XD, XO = side + up, side + down, side + far
    channels = pl.ds(pl.multiple_of(m * 32, 32), 32)

    def rows_of(index, count):
        return pl.ds(pl.multiple_of(index * count, count), count)

    def remote(src, dst, send, recv, dp, space):
        return pltpu.make_async_remote_copy(
            src_ref=src, dst_ref=dst, send_sem=send, recv_sem=recv, device_id=(dp, space), device_id_type=MESH
        )

    def each(count, body, start=0):
        def step(i, carry):
            body(i)
            return carry

        lax.fori_loop(start, count, step, 0)

    barrier = pltpu.get_barrier_semaphore()

    def greet(dp, space):
        pl.semaphore_signal(barrier, inc=1, device_id=(dp, space), device_id_type=MESH)

    each(8, lambda r: greet(2 * lax.rem(m + r, 8) + e, s), 1)
    each(8, lambda r: greet(d, 2 * lax.rem(z + r, 8) + xh), 1)
    greet(sibling, s)
    greet(d, above)
    greet(d, below)

    pairs = [(x_hbm, x_ref), (g_hbm, g_ref), (w1_hbm, w1.at[e]), (w2_hbm, w2.at[e])]
    loads = [pltpu.make_async_copy(src, dst, in_sem.at[i]) for i, (src, dst) in enumerate(pairs)]
    for load in loads:
        load.start()

    def block(phase, t, chip):
        if phase == 0:
            return ga.at[chip // 2, t, :, pl.ds(pl.multiple_of(lax.rem(chip, 2) * 128, 128), 128)]
        return gb.at[t, :, rows_of(chip, 32), :]

    HOPS = [(m, X, X), (m, U, D), (m, D, U), (m, O, O), (X, U, XD), (X, D, XU), (O, X, XO)]

    def hop(phase, t, kind):
        chip, to, _ = HOPS[kind]
        ref = block(phase, t, chip)
        return remote(ref, ref, a_send.at[phase, t, kind], a_recv.at[phase, t, kind], 2 * to + e, s)

    def landed(phase, t, *kinds):
        for kind in kinds:
            _, to, chip = HOPS[kind]
            ref = block(phase, t, chip)
            remote(ref, ref, a_send.at[phase, t, kind], a_recv.at[phase, t, kind], 2 * to + e, s).wait_recv()

    def depart(phase, t):
        for kind in range(4):
            hop(phase, t, kind).start()

    def relay(phase, t):
        landed(phase, t, 0)
        hop(phase, t, 4).start()
        hop(phase, t, 5).start()
        landed(phase, t, 3)
        hop(phase, t, 6).start()

    def slices(which, src, r, to, source):
        return remote(
            src.at[pl.ds(2 * to, 2)], r.at[:, source, e], w_send.at[which, to], w_recv.at[which, source], 2 * to + e, s
        )

    def cores(index, src, dst):
        return remote(src, dst, v_send.at[index], v_recv.at[index], sibling, s)

    def send_slices(which, src, r):
        each(8, lambda step: slices(which, src, r, lax.rem(m + step, 8), m).start(), 1)
        for slot in range(2):
            r[slot, m, e] = src[2 * m + slot]

    def pass_slices(which, src, r):
        def body(step):
            at = lax.rem(m + 8 - step, 8)
            slices(which, src, r, at, at).wait_recv()

        each(8, body, 1)
        cores(which, r.at[:, :, e], r.at[:, :, e]).start()

    def wait_slices(which, r, f):
        cores(which, r.at[:, :, 1 - e], r.at[:, :, 1 - e]).wait_recv()
        for slot in range(2):
            f[slot] = r[slot].reshape(C, 512).astype(F32).T.astype(BF16)

    mine_at = pl.ds(pl.multiple_of(lax.rem(m, 2) * 128, 128), 128)
    loads[0].wait()
    ga[m // 2, 0, :, mine_at] = x_ref[...].astype(F32).T.astype(BF16)
    loads[1].wait()
    ga[m // 2, 1, :, mine_at] = g_ref[...].astype(F32).T.astype(BF16)
    loads[2].wait()
    regroup(w1.at[e], z1)
    loads[3].wait()
    regroup(w2.at[e], z2)
    sent[:, TILES:] = jnp.zeros((2, 8 * SHARE - TILES, 16, 128), BF16)
    mine[:, TILES:] = jnp.zeros((2, 8 * SHARE - TILES, 16, 128), F32)
    pl.semaphore_wait(barrier, 17)

    depart(0, 0)
    send_slices(0, z1, r1)
    depart(0, 1)
    cores(2, w2.at[e], w2.at[e]).start()
    cores(3, w1.at[e], w1.at[e]).start()
    landed(0, 0, 0)
    hop(0, 0, 4).start()
    hop(0, 0, 5).start()
    pass_slices(0, z1, r1)
    landed(0, 0, 3)
    hop(0, 0, 6).start()
    relay(0, 1)
    wait_slices(0, r1, f1)
    cores(2, w2.at[1 - e], w2.at[1 - e]).wait_recv()

    def halo_copies(phase, pair):
        return (
            remote(hm.at[phase, pair], rhm.at[phase, pair], h_send.at[phase, 0, pair], h_recv.at[phase, 0, pair], d, below),
            remote(hp.at[phase, pair], rhp.at[phase, pair], h_send.at[phase, 1, pair], h_recv.at[phase, 1, pair], d, above),
        )

    own_pair, other_pair = xl * 2 + y // 2, xl * 2 + 1 - y // 2
    ORDER = [own_pair, other_pair, side // 2 + y // 2, side // 2 + 1 - y // 2]

    def pair_at(i):
        pair = ORDER[0]
        for at in range(1, 4):
            pair = jnp.where(i == at, ORDER[at], pair)
        return pair

    def convolve(phase, pair, f, v, w, g):
        for slot in range(2):
            rows = pl.ds(16 * slot, 16)
            for t in range(2):
                y = y_ref.at[2 * slot + t]
                y[...] = dot(f[slot, :ROWS], v()) if t == 0 else dot(w[slot], g())
                gather_taps(
                    y, p_ref.at[t, pair, rows], hm.at[phase, pair, t, rows], hp.at[phase, pair, t, rows], 1 - 2 * t
                )
        for copy in halo_copies(phase, pair):
            copy.start()

    def phase_one(i):
        for at, kinds in enumerate(((1, 2), (3,), (0, 4, 5), (6,))):
            @pl.when(i == at)
            def _():
                for t in range(2):
                    landed(0, t, *[kind for kind in kinds if kind not in (0, 3)])

        pair = pair_at(i)
        convolve(0, pair, f1, lambda: ga[pair, 0], w2, lambda: ga[pair, 1])

    each(4, phase_one)
    send_slices(1, z2, r2)

    def near(index, src, dst, to):
        return remote(src, dst, n_send.at[index], n_recv.at[index], d, to)

    def x_edges(pair):
        lowest, highest = edge_planes(ga[pair, 0, channels, :].astype(F32))
        xm[pair] = lowest.astype(BF16)
        xp[pair] = highest.astype(BF16)

    each(4, x_edges)

    def halo_of(phase, t, pair):
        return jnp.concatenate(spread_halo(rhp[phase, pair, t], rhm[phase, pair, t], first, final), axis=1)

    def middle(i):
        pair = pair_at(i)
        for copy in halo_copies(0, pair):
            copy.wait_recv()
        pre = p_ref[0, pair] + halo_of(0, 0, pair)
        grad = p_ref[1, pair] + halo_of(0, 1, pair)
        sig = jax.nn.sigmoid(pre)
        act = (pre * sig).astype(BF16)
        gb[0, pair, channels, :] = act
        gb[1, pair, channels, :] = (grad * sig * (1.0 + pre * (1.0 - sig))).astype(BF16)
        lowest, highest = edge_planes(act.astype(F32))
        am[pair] = lowest.astype(BF16)
        ap[pair] = highest.astype(BF16)

    each(4, middle)
    depart(1, 1)
    near(2, am, ram, below).start()
    near(3, ap, rap, above).start()
    depart(1, 0)
    near(0, xm, rxm, below).start()
    near(1, xp, rxp, above).start()

    def taps(pair, v, up_halo, down_halo, im):
        for slot in range(2):
            rows = slice(16 * slot, 16 * slot + 16)
            halos = spread_halo(up_halo[pair, rows], down_halo[pair, rows], first, final)
            scatter_taps(v[rows], halos, im.at[pair, slot])

    def taps_x(pair):
        taps(pair, ga[pair, 0, channels, :].astype(F32), rxp, rxm, imx)

    def taps_a(pair):
        taps(pair, gb[0, pair, channels, :].astype(F32), rap, ram, ima)

    def core_copy(which):
        return remote(gout.at[which], gin2.at[which], c_send.at[which], c_recv.at[which], sibling, s)

    def reduce_copy(which, step):
        to = lax.rem(z + step, 8)
        return remote(
            sent.at[which, pl.ds(to * SHARE, SHARE)], rr.at[which, step],
            r_send.at[which, step], r_recv.at[which, step], d, 2 * to + xh,
        )

    def product(im, slot, operand, total):
        total[...] = dot(im[0, slot], operand(0), ((1,), (1,)))

        def add(pair):
            total[...] += dot(im[pair, slot], operand(pair), ((1,), (1,)))

        each(4, add, 1)

    def send_partial(which, im, operand):
        product(im, 1 - e, operand, gout.at[which])
        core_copy(which).start()
        product(im, e, operand, gsum)
        core_copy(which).wait_recv()
        for tile in range(TILES):
            row, lane = tile // 2 * 16, tile % 2 * 128
            at = (slice(row, row + 16), slice(lane, lane + 128))
            value = gsum[at] + gin2[(which, *at)]
            mine[which, tile] = value
            sent[which, tile] = value.astype(BF16)
        each(8, lambda step: reduce_copy(which, step).start(), 1)

    def pair_copy(which):
        return remote(part.at[which], other.at[which], x_send.at[which], x_recv.at[which], d, 2 * z + 1 - xh)

    def reduce_ring(which):
        each(8, lambda step: reduce_copy(which, step).wait_recv(), 1)
        total = mine[which, pl.ds(z * SHARE, SHARE)]
        for step in range(1, 8):
            total += rr[which, step].astype(F32)
        part[which] = total
        pair_copy(which).start()

    CUT = SHARE // 2 + 1
    STEPS = [
        (0, 0, SHARE, 2), (0, 0, SHARE, -2),
        (-2, 0, SHARE, -1), (-2, 0, SHARE, 1), (2, 0, SHARE, 1), (2, 0, SHARE, -1),
        (-2, 0, CUT, 2), (2, CUT, SHARE, -2),
    ]

    def spread_copy(which, kind, arriving=False):
        owner, low, high, far_to = STEPS[kind]
        if arriving:
            owner = owner - far_to
        ref = full.at[which, pl.ds(lax.rem(z + owner + 8, 8) * SHARE + low, high - low)]
        to = 2 * lax.rem(z + far_to + 8, 8) + xh
        return remote(ref, ref, f_send.at[which, kind], f_recv.at[which, kind], d, to)

    def spread(which):
        pair_copy(which).wait_recv()
        full[which, pl.ds(z * SHARE, SHARE)] = (part[which] + other[which]) * factor
        spread_copy(which, 0).start()
        spread_copy(which, 1).start()

    def spread_on(which):
        for kind, then in ((0, (3, 2, 6)), (1, (5, 4, 7))):
            spread_copy(which, kind, True).wait_recv()
            for more in then:
                spread_copy(which, more).start()

    def gradient_out(which, ref):
        for kind in range(2, 8):
            spread_copy(which, kind, True).wait_recv()
        for tile in range(TILES):
            row, lane = tile // 2 * 16, tile % 2 * 128
            ref[row : row + 16, lane : lane + 128] = full[which, tile]

    relay(1, 1)
    near(2, am, ram, below).wait_recv()
    near(3, ap, rap, above).wait_recv()
    each(4, taps_a)
    relay(1, 0)
    send_partial(1, ima, lambda pair: ga[pair, 1])
    near(0, xm, rxm, below).wait_recv()
    near(1, xp, rxp, above).wait_recv()
    each(4, taps_x)
    landed(1, 1, 1, 2, 4, 5, 6)
    send_partial(0, imx, lambda pair: gb[1, pair])
    pass_slices(1, z2, r2)
    reduce_ring(1)
    landed(1, 0, 1, 2, 4, 5, 6)
    wait_slices(1, r2, f2)
    cores(3, w1.at[1 - e], w1.at[1 - e]).wait_recv()

    def phase_two(i):
        @pl.when(i == 2)
        def _():
            spread(1)

        pair = pair_at(i)
        convolve(1, pair, f2, lambda: gb[0, pair], w1, lambda: gb[1, pair])

    each(4, phase_two)
    reduce_ring(0)
    spread_on(1)

    def home(to, source):
        return remote(oc.at[to], oall.at[source], o_send.at[to], o_recv.at[source], 2 * to + e, s)

    def finish(i):
        pair = pair_at(i)
        for copy in halo_copies(1, pair):
            copy.wait_recv()
        for t in range(2):
            total = p_ref[t, pair] + halo_of(1, t, pair)
            total = (ga[pair, t, channels, :].astype(F32) + total).astype(BF16)
            oc[2 * pair, t] = total[:, :128]
            oc[2 * pair + 1, t] = total[:, 128:]
        for half in range(2):
            to = 2 * pair + half

            @pl.when(to != m)
            def _():
                home(to, m).start()

    each(4, finish)
    spread(0)
    oall[m] = oc[m]

    def wait_home(step):
        source = lax.rem(m + 8 - step, 8)
        home(source, source).wait_recv()

    each(8, wait_home, 1)
    out_ref[...] = oall[:, 0].reshape(C, 128).astype(F32).T.astype(BF16)
    gin_ref[...] = oall[:, 1].reshape(C, 128).astype(F32).T.astype(BF16)
    spread_on(0)
    gradient_out(1, two_ref)
    gradient_out(0, one_ref)

    def wait_far(step):
        to = lax.rem(m + step, 8)
        home(to, m).wait_send()
        slices(0, z1, r1, to, m).wait_send()
        slices(1, z2, r2, to, m).wait_send()
        for which in range(2):
            reduce_copy(which, step).wait_send()

    each(8, wait_far, 1)

    def wait_halo(pair):
        for phase in range(2):
            for copy in halo_copies(phase, pair):
                copy.wait_send()

    each(4, wait_halo)
    cores(0, r1.at[:, :, e], r1.at[:, :, e]).wait_send()
    cores(1, r2.at[:, :, e], r2.at[:, :, e]).wait_send()
    cores(2, w2.at[e], w2.at[e]).wait_send()
    cores(3, w1.at[e], w1.at[e]).wait_send()
    for t in range(2):
        core_copy(t).wait_send()
        pair_copy(t).wait_send()
        for kind in range(8):
            spread_copy(t, kind).wait_send()
        for phase in range(2):
            for kind in range(7):
                hop(phase, t, kind).wait_send()
    near(0, xm, rxm, below).wait_send()
    near(1, xp, rxp, above).wait_send()
    near(2, am, ram, below).wait_send()
    near(3, ap, rap, above).wait_send()


def shards(features, weight_one, weight_two, cotangent):
    shape = features.shape
    count = shape[0] * lax.axis_size("dp") * shape[1] * lax.axis_size("space") * shape[2] * shape[3]
    factor = float(count) ** (-0.5)
    vmem = pl.BlockSpec(memory_space=pltpu.VMEM)
    dma = pltpu.SemaphoreType.DMA
    scratch = pltpu.VMEM
    out, gin, one, two = pl.pallas_call(
        functools.partial(kernel, factor),
        out_shape=[
            jax.ShapeDtypeStruct((128, C), BF16),
            jax.ShapeDtypeStruct((128, C), BF16),
            jax.ShapeDtypeStruct((ROWS, C), F32),
            jax.ShapeDtypeStruct((ROWS, C), F32),
        ],
        in_specs=[pl.BlockSpec(memory_space=pl.ANY)] * 4,
        out_specs=[vmem] * 4,
        scratch_shapes=[
            scratch((128, C), BF16), scratch((128, C), BF16),
            scratch((2, ROWS, C), BF16), scratch((2, ROWS, C), BF16),
            scratch((4, 2, C, C), BF16),
            scratch((2, 4, C, C), BF16),
            scratch((16, 16, 512), BF16), scratch((16, 16, 512), BF16),
            scratch((2, 8, 2, 16, 512), BF16), scratch((2, 8, 2, 16, 512), BF16),
            scratch((2, 512, C), BF16), scratch((2, 512, C), BF16),
            scratch((4, ROWS, C), F32),
            scratch((2, 4, 32, C), F32),
            *[scratch((2, 4, 2, 32, 128), F32)] * 4,
            *[scratch((4, 32, 128), BF16)] * 8,
            scratch((4, 2, ROWS, C), BF16), scratch((4, 2, ROWS, C), BF16),
            scratch((ROWS, C), F32),
            scratch((2, ROWS, C), F32), scratch((2, ROWS, C), F32),
            scratch((2, 8 * SHARE, 16, 128), F32),
            scratch((2, 8 * SHARE, 16, 128), BF16),
            scratch((2, 8, SHARE, 16, 128), BF16),
            scratch((2, SHARE, 16, 128), F32), scratch((2, SHARE, 16, 128), F32),
            scratch((2, 8 * SHARE, 16, 128), F32),
            scratch((8, 2, 32, 128), BF16), scratch((8, 2, 32, 128), BF16),
            dma((4,)),
            dma((2, 8)), dma((2, 8)), dma((4,)), dma((4,)),
            dma((2, 2, 7)), dma((2, 2, 7)),
            dma((2, 2, 4)), dma((2, 2, 4)),
            dma((4,)), dma((4,)), dma((2,)), dma((2,)),
            dma((2, 8)), dma((2, 8)), dma((2,)), dma((2,)), dma((2, 8)), dma((2, 8)),
            dma((8,)), dma((8,)),
        ],
        compiler_params=pltpu.CompilerParams(
            collective_id=0, has_side_effects=True, vmem_limit_bytes=56 * 2**20
        ),
    )(
        features.reshape(128, C), cotangent.reshape(128, C),
        weight_one.reshape(ROWS, C), weight_two.reshape(ROWS, C),
    )
    return out.reshape(shape), gin.reshape(shape), one.reshape(TAPS, 16, C), two.reshape(TAPS, 16, C)


def solution(mesh):
    in_specs = (
        P("dp", "space", None, None, None),
        P(None, "dp", None),
        P(None, "dp", None),
        P("dp", "space", None, None, None),
    )
    out_specs = (
        P("dp", "space", None, None, None),
        P("dp", "space", None, None, None),
        P(None, "dp", None),
        P(None, "dp", None),
    )
    return jax.shard_map(shards, mesh=mesh, in_specs=in_specs, out_specs=out_specs, check_vma=False)
```

```python
import functools

import jax
import jax.numpy as jnp
from jax import lax
from jax.experimental import pallas as pl
from jax.experimental.pallas import tpu as pltpu
from jax.sharding import PartitionSpec as P

MESH = pl.DeviceIdType.MESH
F32 = jnp.float32
BF16 = jnp.bfloat16
C = 256
TAPS = 27
ROWS = TAPS * 16
TILES = 2 * TAPS
SHARE = -(-TILES // 8)


def dot(a, b, dims=((1,), (0,))):
    return lax.dot_general(a, b, (dims, ((), ())), preferred_element_type=F32)


def lanes():
    return lax.broadcasted_iota(jnp.int32, (16, 128), 1)


def lower(rows=16):
    return lax.broadcasted_iota(jnp.int32, (rows, 128), 1) < 64


def half_turn(v):
    return pltpu.roll(v, 64, 1)


def inside(j, k, sign):
    lane = lanes()
    y = (lane // 8) % 8 + sign * (j - 1)
    z = lane % 8 + sign * (k - 1)
    return (y >= 0) & (y < 8) & (z >= 0) & (z < 8)


def shifted(v, j, k, sign):
    delta = sign * (8 * (j - 1) + (k - 1))
    if delta == 0:
        return v
    parts = v.shape[0] // 16
    keep = inside(j, k, sign)
    if parts > 1:
        keep = jnp.concatenate([keep] * parts, axis=0)
    return jnp.where(keep, pltpu.roll(v, (-delta) % 128, 1), 0.0)


def regroup(w_ref, z_ref):
    group = lanes() // 16
    for q in range(4):
        for h in range(2):
            tiles = []
            for i in range(8):
                tap = 8 * q + i
                if tap < TAPS:
                    tiles.append(w_ref[16 * tap : 16 * tap + 16, 128 * h : 128 * h + 128].astype(F32))
                else:
                    tiles.append(jnp.zeros((16, 128), F32))
            for bit in (1, 2, 4):
                low = (group & bit) == 0
                for i in range(8):
                    if i & bit:
                        continue
                    a, b = tiles[i], tiles[i + bit]
                    tiles[i] = jnp.where(low, a, pltpu.roll(b, 16 * bit, 1))
                    tiles[i + bit] = jnp.where(low, pltpu.roll(a, 128 - 16 * bit, 1), b)
            for i in range(8):
                z_ref[8 * h + i, :, 128 * q : 128 * q + 128] = tiles[i].astype(BF16)


def gather_taps(y_ref, p_ref, hm_ref, hp_ref, sign):
    lo = lower()
    lefts = []
    for half in range(2):
        at = slice(128 * half, 128 * half + 128)
        total = None
        for j in range(3):
            for k in range(3):
                rows = [16 * (9 * i + 3 * j + k) for i in range(3)]
                first, mid, last = [y_ref[r : r + 16, at] for r in rows]
                if sign < 0:
                    first, last = last, first
                inner = jnp.where(lo, first, last)
                outer = jnp.where(lo, last, first)
                term = shifted(jnp.concatenate([mid, inner, outer], axis=0), j, k, sign)
                total = term if total is None else total + term
        p_ref[:, at] = total[:16] + half_turn(total[16:32])
        lefts.append(total[32:])
    hm_ref[...] = jnp.where(lo, lefts[0], half_turn(lefts[1]))
    hp_ref[...] = jnp.where(lo, half_turn(lefts[0]), lefts[1])


def spread_halo(hp, hm, first, final):
    lo = lower(hp.shape[0])
    hp = jnp.where(first, 0.0, hp.astype(F32))
    hm = jnp.where(final, 0.0, hm.astype(F32))
    return [jnp.where(lo, hp, half_turn(hm)), jnp.where(lo, half_turn(hp), hm)]


def edge_planes(v):
    lo = lower(v.shape[0])
    a, b = v[:, :128], v[:, 128:]
    return jnp.where(lo, a, half_turn(b)), jnp.where(lo, half_turn(a), b)


def scatter_taps(v, halos, im_ref):
    lo = lower()
    for half in range(2):
        at = slice(128 * half, 128 * half + 128)
        own = v[:, at]
        turned = half_turn(own)
        stack = jnp.concatenate(
            [jnp.where(lo, halos[half], turned), own, jnp.where(lo, turned, halos[half])], axis=0
        )
        for j in range(3):
            for k in range(3):
                term = shifted(stack, j, k, 1).astype(BF16)
                for i in range(3):
                    row = 16 * (9 * i + 3 * j + k)
                    im_ref[row : row + 16, at] = term[16 * i : 16 * i + 16]


def kernel(
    factor,
    x_hbm, g_hbm, w1_hbm, w2_hbm,
    cells_hbm, grads_hbm,
    x_ref, g_ref, w1, w2,
    ga, gb, z1, z2, r1, r2, f1, f2, y_ref, p_ref, hm, hp, rhm, rhp,
    xm, xp, rxm, rxp, am, ap, ram, rap, imx, ima, gsum, gout, gin2, mine, sent, rr, part, other, full, oc, oall,
    in_sem, out_sem, w_send, w_recv, v_send, v_recv, a_send, a_recv,
    h_send, h_recv, n_send, n_recv, c_send, c_recv, r_send, r_recv, x_send, x_recv, f_send, f_recv, o_send, o_recv,
):
    d = lax.axis_index("dp")
    s = lax.axis_index("space")
    m, e = d // 2, d % 2
    xl, y = m // 4, m % 4
    z, xh = s // 2, s % 2
    above = lax.rem(s + 1, 16)
    below = lax.rem(s + 15, 16)
    first, final = s == 0, s == 15
    sibling = 2 * m + 1 - e
    across = 2 * z + 1 - xh
    up, down, far = [lax.rem(y + step, 4) for step in (1, 3, 2)]
    side = (1 - xl) * 4
    U, D, O, X = xl * 4 + up, xl * 4 + down, xl * 4 + far, side + y
    XU, XD, XO = side + up, side + down, side + far
    channels = pl.ds(pl.multiple_of(m * 32, 32), 32)

    def rows_of(index, count):
        return pl.ds(pl.multiple_of(index * count, count), count)

    def remote(src, dst, send, recv, dp, space):
        return pltpu.make_async_remote_copy(
            src_ref=src, dst_ref=dst, send_sem=send, recv_sem=recv, device_id=(dp, space), device_id_type=MESH
        )

    def each(count, body, start=0):
        def step(i, carry):
            body(i)
            return carry

        lax.fori_loop(start, count, step, 0)

    barrier = pltpu.get_barrier_semaphore()

    def greet(dp, space):
        pl.semaphore_signal(barrier, inc=1, device_id=(dp, space), device_id_type=MESH)

    each(8, lambda r: greet(2 * lax.rem(m + r, 8) + e, s), 1)
    each(8, lambda r: greet(d, 2 * lax.rem(z + r, 8) + xh), 1)
    greet(sibling, s)
    greet(d, above)
    greet(d, below)
    each(4, lambda r: greet(2 * (side + r) + e, across))

    pairs = [(x_hbm, x_ref), (g_hbm, g_ref), (w1_hbm, w1.at[e]), (w2_hbm, w2.at[e])]
    loads = [pltpu.make_async_copy(src, dst, in_sem.at[i]) for i, (src, dst) in enumerate(pairs)]
    for load in loads:
        load.start()

    def block(phase, t, chip):
        if phase == 0:
            return ga.at[chip // 2, t, :, pl.ds(pl.multiple_of(lax.rem(chip, 2) * 128, 128), 128)]
        return gb.at[t, :, rows_of(chip, 32), :]

    HOPS = [
        (m, None, X, X), (m, None, U, D), (m, None, D, U), (X, None, U, XD), (X, None, D, XU),
        (D, 0, U, O), (U, 1, D, O), (XD, 0, U, XO), (XU, 1, D, XO),
    ]

    def hop(phase, t, kind, arriving=False):
        chip, half, to, source = HOPS[kind]
        ref = block(phase, t, source if arriving else chip)
        if half is not None:
            ref = ref.at[pl.ds(128 * half, 128)] if phase == 0 else ref.at[pl.ds(2 * half, 2)]
        return remote(ref, ref, a_send.at[phase, t, kind], a_recv.at[phase, t, kind], 2 * to + e, s)

    def landed(phase, t, *kinds):
        for kind in kinds:
            hop(phase, t, kind, True).wait_recv()

    def depart(phase, t):
        for kind in range(3):
            hop(phase, t, kind).start()

    def relay(phase, t):
        for kind, then in ((0, (3, 4)), (1, (5,)), (2, (6,))):
            landed(phase, t, kind)
            for more in then:
                hop(phase, t, more).start()

    def relay_more(phase, t):
        for kind, more in ((3, 7), (4, 8)):
            landed(phase, t, kind)
            hop(phase, t, more).start()

    def slices(which, src, r, to, source):
        space = jnp.where(to // 4 == xl, s, across)
        return remote(
            src.at[pl.ds(2 * to, 2)], r.at[:, source, e],
            w_send.at[which, to], w_recv.at[which, source], 2 * to + e, space,
        )

    def cores(index, src, dst):
        return remote(src, dst, v_send.at[index], v_recv.at[index], sibling, s)

    def send_slices(which, src, r):
        each(8, lambda step: slices(which, src, r, lax.rem(m + step, 8), m).start(), 1)
        for slot in range(2):
            r[slot, m, e] = src[2 * m + slot]

    def pass_slices(which, src, r):
        def body(step):
            at = lax.rem(m + 8 - step, 8)
            slices(which, src, r, at, at).wait_recv()

        each(8, body, 1)
        cores(which, r.at[:, :, e], r.at[:, :, e]).start()

    def wait_slices(which, r, f):
        cores(which, r.at[:, :, 1 - e], r.at[:, :, 1 - e]).wait_recv()
        for slot in range(2):
            f[slot] = r[slot].reshape(C, 512).astype(F32).T.astype(BF16)

    mine_at = pl.ds(pl.multiple_of(lax.rem(m, 2) * 128, 128), 128)
    loads[0].wait()
    ga[m // 2, 0, :, mine_at] = x_ref[...].astype(F32).T.astype(BF16)
    loads[1].wait()
    ga[m // 2, 1, :, mine_at] = g_ref[...].astype(F32).T.astype(BF16)
    loads[2].wait()
    regroup(w1.at[e], z1)
    loads[3].wait()
    regroup(w2.at[e], z2)
    sent[:, TILES:] = jnp.zeros((2, 8 * SHARE - TILES, 16, 128), BF16)
    mine[:, TILES:] = jnp.zeros((2, 8 * SHARE - TILES, 16, 128), F32)
    pl.semaphore_wait(barrier, 21)

    depart(0, 0)
    send_slices(0, z1, r1)
    depart(0, 1)
    cores(2, w2.at[e], w2.at[e]).start()
    relay(0, 0)
    pass_slices(0, z1, r1)
    relay(0, 1)
    relay_more(0, 0)
    wait_slices(0, r1, f1)
    cores(2, w2.at[1 - e], w2.at[1 - e]).wait_recv()

    def halo_copies(phase, pair):
        return (
            remote(hm.at[phase, pair], rhm.at[phase, pair], h_send.at[phase, 0, pair], h_recv.at[phase, 0, pair], d, below),
            remote(hp.at[phase, pair], rhp.at[phase, pair], h_send.at[phase, 1, pair], h_recv.at[phase, 1, pair], d, above),
        )

    own_pair, other_pair = xl * 2 + y // 2, xl * 2 + 1 - y // 2
    ORDER = [own_pair, other_pair, side // 2 + y // 2, side // 2 + 1 - y // 2]

    def pair_at(i):
        pair = ORDER[0]
        for at in range(1, 4):
            pair = jnp.where(i == at, ORDER[at], pair)
        return pair

    def convolve(phase, pair, f, v, w, g):
        for slot in range(2):
            rows = pl.ds(16 * slot, 16)
            for t in range(2):
                y = y_ref.at[2 * slot + t]
                y[...] = dot(f[slot, :ROWS], v()) if t == 0 else dot(w[slot], g())
                gather_taps(
                    y, p_ref.at[t, pair, rows], hm.at[phase, pair, t, rows], hp.at[phase, pair, t, rows], 1 - 2 * t
                )
        for copy in halo_copies(phase, pair):
            copy.start()

    def phase_one(i):
        for at, kinds in ((1, (5, 6)), (3, (7, 8))):
            @pl.when(i == at)
            def _():
                if at == 1:
                    relay_more(0, 1)
                for t in range(2):
                    landed(0, t, *kinds)

        pair = pair_at(i)
        convolve(0, pair, f1, lambda: ga[pair, 0], w2, lambda: ga[pair, 1])

    each(4, phase_one)
    cores(3, w1.at[e], w1.at[e]).start()
    send_slices(1, z2, r2)

    def near(index, src, dst, to):
        return remote(src, dst, n_send.at[index], n_recv.at[index], d, to)

    def x_edges(pair):
        lowest, highest = edge_planes(ga[pair, 0, channels, :].astype(F32))
        xm[pair] = lowest.astype(BF16)
        xp[pair] = highest.astype(BF16)

    each(4, x_edges)

    def halo_of(phase, t, pair):
        return jnp.concatenate(spread_halo(rhp[phase, pair, t], rhm[phase, pair, t], first, final), axis=1)

    def middle(i):
        pair = pair_at(i)
        for copy in halo_copies(0, pair):
            copy.wait_recv()
        pre = p_ref[0, pair] + halo_of(0, 0, pair)
        grad = p_ref[1, pair] + halo_of(0, 1, pair)
        sig = jax.nn.sigmoid(pre)
        act = (pre * sig).astype(BF16)
        gb[0, pair, channels, :] = act
        gb[1, pair, channels, :] = (grad * sig * (1.0 + pre * (1.0 - sig))).astype(BF16)
        lowest, highest = edge_planes(act.astype(F32))
        am[pair] = lowest.astype(BF16)
        ap[pair] = highest.astype(BF16)

    each(4, middle)
    depart(1, 1)
    near(2, am, ram, below).start()
    near(3, ap, rap, above).start()
    depart(1, 0)
    near(0, xm, rxm, below).start()
    near(1, xp, rxp, above).start()

    def taps(pair, v, up_halo, down_halo, im):
        for slot in range(2):
            rows = slice(16 * slot, 16 * slot + 16)
            halos = spread_halo(up_halo[pair, rows], down_halo[pair, rows], first, final)
            scatter_taps(v[rows], halos, im.at[pair, slot])

    def taps_x(pair):
        taps(pair, ga[pair, 0, channels, :].astype(F32), rxp, rxm, imx)

    def taps_a(pair):
        taps(pair, gb[0, pair, channels, :].astype(F32), rap, ram, ima)

    def core_copy(which):
        return remote(gout.at[which], gin2.at[which], c_send.at[which], c_recv.at[which], sibling, s)

    def reduce_copy(which, step):
        to = lax.rem(z + step, 8)
        return remote(
            sent.at[which, pl.ds(to * SHARE, SHARE)], rr.at[which, step],
            r_send.at[which, step], r_recv.at[which, step], d, 2 * to + xh,
        )

    def product(im, slot, operand, total):
        total[...] = dot(im[0, slot], operand(0), ((1,), (1,)))

        def add(pair):
            total[...] += dot(im[pair, slot], operand(pair), ((1,), (1,)))

        each(4, add, 1)

    def send_partial(which, im, operand):
        product(im, 1 - e, operand, gout.at[which])
        core_copy(which).start()
        product(im, e, operand, gsum)
        core_copy(which).wait_recv()
        for tile in range(TILES):
            row, lane = tile // 2 * 16, tile % 2 * 128
            at = (slice(row, row + 16), slice(lane, lane + 128))
            value = gsum[at] + gin2[(which, *at)]
            mine[which, tile] = value
            sent[which, tile] = value.astype(BF16)
        each(8, lambda step: reduce_copy(which, step).start(), 1)

    def pair_copy(which):
        return remote(part.at[which], other.at[which], x_send.at[which], x_recv.at[which], d, 2 * z + 1 - xh)

    def reduce_ring(which):
        each(8, lambda step: reduce_copy(which, step).wait_recv(), 1)
        total = mine[which, pl.ds(z * SHARE, SHARE)]
        for step in range(1, 8):
            total += rr[which, step].astype(F32)
        part[which] = total
        pair_copy(which).start()

    CUT = SHARE // 2 + 1
    STEPS = [
        (0, 0, SHARE, 2), (0, 0, SHARE, -2),
        (-2, 0, SHARE, -1), (-2, 0, SHARE, 1), (2, 0, SHARE, 1), (2, 0, SHARE, -1),
        (-2, 0, CUT, 2), (2, CUT, SHARE, -2),
    ]

    def spread_copy(which, kind, arriving=False):
        owner, low, high, far_to = STEPS[kind]
        if arriving:
            owner = owner - far_to
        ref = full.at[which, pl.ds(lax.rem(z + owner + 8, 8) * SHARE + low, high - low)]
        to = 2 * lax.rem(z + far_to + 8, 8) + xh
        return remote(ref, ref, f_send.at[which, kind], f_recv.at[which, kind], d, to)

    def spread(which):
        pair_copy(which).wait_recv()
        full[which, pl.ds(z * SHARE, SHARE)] = ((part[which] + other[which]) * factor).astype(BF16)
        spread_copy(which, 0).start()
        spread_copy(which, 1).start()

    def spread_on(which):
        for kind, then in ((0, (3, 2, 6)), (1, (5, 4, 7))):
            spread_copy(which, kind, True).wait_recv()
            for more in then:
                spread_copy(which, more).start()

    def result(which):
        src, dst = (oall, cells_hbm) if which == 2 else (full.at[which], grads_hbm.at[which])
        return pltpu.make_async_copy(src, dst, out_sem.at[which])

    def spread_end(which):
        for kind in range(2, 8):
            spread_copy(which, kind, True).wait_recv()
        result(which).start()

    relay(1, 1)
    near(2, am, ram, below).wait_recv()
    near(3, ap, rap, above).wait_recv()
    each(4, taps_a)
    relay(1, 0)
    relay_more(1, 1)
    send_partial(1, ima, lambda pair: ga[pair, 1])
    near(0, xm, rxm, below).wait_recv()
    near(1, xp, rxp, above).wait_recv()
    each(4, taps_x)
    relay_more(1, 0)
    landed(1, 1, 5, 6, 7, 8)
    send_partial(0, imx, lambda pair: gb[1, pair])
    pass_slices(1, z2, r2)
    landed(1, 0, 5, 6, 7, 8)
    wait_slices(1, r2, f2)
    cores(3, w1.at[1 - e], w1.at[1 - e]).wait_recv()

    def phase_two(i):
        @pl.when(i == 2)
        def _():
            reduce_ring(1)

        pair = pair_at(i)
        convolve(1, pair, f2, lambda: gb[0, pair], w1, lambda: gb[1, pair])

    each(4, phase_two)
    spread(1)
    reduce_ring(0)

    def home(to, source):
        return remote(oc.at[to], oall.at[source], o_send.at[to], o_recv.at[source], 2 * to + e, s)

    def finish(i):
        pair = pair_at(i)
        for copy in halo_copies(1, pair):
            copy.wait_recv()
        for t in range(2):
            total = p_ref[t, pair] + halo_of(1, t, pair)
            total = (ga[pair, t, channels, :].astype(F32) + total).astype(BF16)
            oc[2 * pair, t] = total[:, :128]
            oc[2 * pair + 1, t] = total[:, 128:]
        for half in range(2):
            to = 2 * pair + half

            @pl.when(to != m)
            def _():
                home(to, m).start()

    each(4, finish)
    spread(0)
    spread_on(1)
    oall[m] = oc[m]

    def wait_home(step):
        source = lax.rem(m + 8 - step, 8)
        home(source, source).wait_recv()

    each(8, wait_home, 1)
    result(2).start()
    spread_on(0)
    spread_end(1)
    spread_end(0)
    for which in range(3):
        result(which).wait()

    def wait_far(step):
        to = lax.rem(m + step, 8)
        home(to, m).wait_send()
        slices(0, z1, r1, to, m).wait_send()
        slices(1, z2, r2, to, m).wait_send()
        for which in range(2):
            reduce_copy(which, step).wait_send()

    each(8, wait_far, 1)

    def wait_halo(pair):
        for phase in range(2):
            for copy in halo_copies(phase, pair):
                copy.wait_send()

    each(4, wait_halo)
    cores(0, r1.at[:, :, e], r1.at[:, :, e]).wait_send()
    cores(1, r2.at[:, :, e], r2.at[:, :, e]).wait_send()
    cores(2, w2.at[e], w2.at[e]).wait_send()
    cores(3, w1.at[e], w1.at[e]).wait_send()
    for t in range(2):
        core_copy(t).wait_send()
        pair_copy(t).wait_send()
        for kind in range(8):
            spread_copy(t, kind).wait_send()
        for phase in range(2):
            for kind in range(9):
                hop(phase, t, kind).wait_send()
    near(0, xm, rxm, below).wait_send()
    near(1, xp, rxp, above).wait_send()
    near(2, am, ram, below).wait_send()
    near(3, ap, rap, above).wait_send()


def lay_out(cells_ref, grads_ref, out_ref, gin_ref, one_ref, two_ref):
    for t, ref in enumerate((out_ref, gin_ref)):
        ref[...] = cells_ref[:, t].reshape(C, 128).astype(F32).T.astype(BF16)
    for which, ref in enumerate((one_ref, two_ref)):
        for tile in range(TILES):
            row, lane = tile // 2 * 16, tile % 2 * 128
            ref[row : row + 16, lane : lane + 128] = grads_ref[which, tile].astype(F32)


def shards(features, weight_one, weight_two, cotangent):
    shape = features.shape
    count = shape[0] * lax.axis_size("dp") * shape[1] * lax.axis_size("space") * shape[2] * shape[3]
    factor = float(count) ** (-0.5)
    vmem = pl.BlockSpec(memory_space=pltpu.VMEM)
    dma = pltpu.SemaphoreType.DMA
    scratch = pltpu.VMEM
    cells, grads = pl.pallas_call(
        functools.partial(kernel, factor),
        out_shape=[
            jax.ShapeDtypeStruct((8, 2, 32, 128), BF16),
            jax.ShapeDtypeStruct((2, 8 * SHARE, 16, 128), BF16),
        ],
        in_specs=[pl.BlockSpec(memory_space=pl.ANY)] * 4,
        out_specs=[pl.BlockSpec(memory_space=pl.ANY)] * 2,
        scratch_shapes=[
            scratch((128, C), BF16), scratch((128, C), BF16),
            scratch((2, ROWS, C), BF16), scratch((2, ROWS, C), BF16),
            scratch((4, 2, C, C), BF16),
            scratch((2, 4, C, C), BF16),
            scratch((16, 16, 512), BF16), scratch((16, 16, 512), BF16),
            scratch((2, 8, 2, 16, 512), BF16), scratch((2, 8, 2, 16, 512), BF16),
            scratch((2, 512, C), BF16), scratch((2, 512, C), BF16),
            scratch((4, ROWS, C), F32),
            scratch((2, 4, 32, C), F32),
            *[scratch((2, 4, 2, 32, 128), F32)] * 4,
            *[scratch((4, 32, 128), BF16)] * 8,
            scratch((4, 2, ROWS, C), BF16), scratch((4, 2, ROWS, C), BF16),
            scratch((ROWS, C), F32),
            scratch((2, ROWS, C), F32), scratch((2, ROWS, C), F32),
            scratch((2, 8 * SHARE, 16, 128), F32),
            scratch((2, 8 * SHARE, 16, 128), BF16),
            scratch((2, 8, SHARE, 16, 128), BF16),
            scratch((2, SHARE, 16, 128), F32), scratch((2, SHARE, 16, 128), F32),
            scratch((2, 8 * SHARE, 16, 128), BF16),
            scratch((8, 2, 32, 128), BF16), scratch((8, 2, 32, 128), BF16),
            dma((4,)), dma((3,)),
            dma((2, 8)), dma((2, 8)), dma((4,)), dma((4,)),
            dma((2, 2, 9)), dma((2, 2, 9)),
            dma((2, 2, 4)), dma((2, 2, 4)),
            dma((4,)), dma((4,)), dma((2,)), dma((2,)),
            dma((2, 8)), dma((2, 8)), dma((2,)), dma((2,)), dma((2, 8)), dma((2, 8)),
            dma((8,)), dma((8,)),
        ],
        compiler_params=pltpu.CompilerParams(
            collective_id=0, has_side_effects=True, vmem_limit_bytes=56 * 2**20
        ),
    )(
        features.reshape(128, C), cotangent.reshape(128, C),
        weight_one.reshape(ROWS, C), weight_two.reshape(ROWS, C),
    )
    out, gin, one, two = pl.pallas_call(
        lay_out,
        out_shape=[
            jax.ShapeDtypeStruct((128, C), BF16),
            jax.ShapeDtypeStruct((128, C), BF16),
            jax.ShapeDtypeStruct((ROWS, C), F32),
            jax.ShapeDtypeStruct((ROWS, C), F32),
        ],
        in_specs=[vmem] * 2,
        out_specs=[vmem] * 4,
    )(cells, grads)
    return out.reshape(shape), gin.reshape(shape), one.reshape(TAPS, 16, C), two.reshape(TAPS, 16, C)


def solution(mesh):
    in_specs = (
        P("dp", "space", None, None, None),
        P(None, "dp", None),
        P(None, "dp", None),
        P("dp", "space", None, None, None),
    )
    out_specs = (
        P("dp", "space", None, None, None),
        P("dp", "space", None, None, None),
        P(None, "dp", None),
        P(None, "dp", None),
    )
    return jax.shard_map(shards, mesh=mesh, in_specs=in_specs, out_specs=out_specs, check_vma=False)
```

```python
import functools

import jax
import jax.numpy as jnp
from jax import lax
from jax.experimental import pallas as pl
from jax.experimental.pallas import tpu as pltpu
from jax.sharding import PartitionSpec as P

MESH = pl.DeviceIdType.MESH
F32 = jnp.float32
BF16 = jnp.bfloat16
C = 256
TAPS = 27
ROWS = TAPS * 16
TILES = 2 * TAPS
SHARE = -(-TILES // 8)


def dot(a, b, dims=((1,), (0,))):
    return lax.dot_general(a, b, (dims, ((), ())), preferred_element_type=F32)


def lanes():
    return lax.broadcasted_iota(jnp.int32, (16, 128), 1)


def lower(rows=16):
    return lax.broadcasted_iota(jnp.int32, (rows, 128), 1) < 64


def half_turn(v):
    return pltpu.roll(v, 64, 1)


def inside(j, k, sign):
    lane = lanes()
    y = (lane // 8) % 8 + sign * (j - 1)
    z = lane % 8 + sign * (k - 1)
    return (y >= 0) & (y < 8) & (z >= 0) & (z < 8)


def shifted(v, j, k, sign):
    delta = sign * (8 * (j - 1) + (k - 1))
    if delta == 0:
        return v
    parts = v.shape[0] // 16
    keep = inside(j, k, sign)
    if parts > 1:
        keep = jnp.concatenate([keep] * parts, axis=0)
    return jnp.where(keep, pltpu.roll(v, (-delta) % 128, 1), 0.0)


def regroup(w_ref, z_ref):
    group = lanes() // 16
    for q in range(4):
        for h in range(2):
            tiles = []
            for i in range(8):
                tap = 8 * q + i
                if tap < TAPS:
                    tiles.append(w_ref[16 * tap : 16 * tap + 16, 128 * h : 128 * h + 128].astype(F32))
                else:
                    tiles.append(jnp.zeros((16, 128), F32))
            for bit in (1, 2, 4):
                low = (group & bit) == 0
                for i in range(8):
                    if i & bit:
                        continue
                    a, b = tiles[i], tiles[i + bit]
                    tiles[i] = jnp.where(low, a, pltpu.roll(b, 16 * bit, 1))
                    tiles[i + bit] = jnp.where(low, pltpu.roll(a, 128 - 16 * bit, 1), b)
            for i in range(8):
                z_ref[8 * h + i, :, 128 * q : 128 * q + 128] = tiles[i].astype(BF16)


def gather_taps(y_ref, p_ref, hm_ref, hp_ref, sign):
    lo = lower()
    lefts = []
    for half in range(2):
        at = slice(128 * half, 128 * half + 128)
        total = None
        for j in range(3):
            for k in range(3):
                rows = [16 * (9 * i + 3 * j + k) for i in range(3)]
                first, mid, last = [y_ref[r : r + 16, at] for r in rows]
                if sign < 0:
                    first, last = last, first
                inner = jnp.where(lo, first, last)
                outer = jnp.where(lo, last, first)
                term = shifted(jnp.concatenate([mid, inner, outer], axis=0), j, k, sign)
                total = term if total is None else total + term
        p_ref[:, at] = total[:16] + half_turn(total[16:32])
        lefts.append(total[32:])
    hm_ref[...] = jnp.where(lo, lefts[0], half_turn(lefts[1])).astype(hm_ref.dtype)
    hp_ref[...] = jnp.where(lo, half_turn(lefts[0]), lefts[1]).astype(hp_ref.dtype)


def spread_halo(hp, hm, first, final):
    lo = lower(hp.shape[0])
    hp = jnp.where(first, 0.0, hp.astype(F32))
    hm = jnp.where(final, 0.0, hm.astype(F32))
    return [jnp.where(lo, hp, half_turn(hm)), jnp.where(lo, half_turn(hp), hm)]


def edge_planes(v):
    lo = lower(v.shape[0])
    a, b = v[:, :128], v[:, 128:]
    return jnp.where(lo, a, half_turn(b)), jnp.where(lo, half_turn(a), b)


def scatter_taps(v, halos, im_ref):
    lo = lower()
    for half in range(2):
        at = slice(128 * half, 128 * half + 128)
        own = v[:, at]
        turned = half_turn(own)
        stack = jnp.concatenate(
            [jnp.where(lo, halos[half], turned), own, jnp.where(lo, turned, halos[half])], axis=0
        )
        for j in range(3):
            for k in range(3):
                term = shifted(stack, j, k, 1).astype(BF16)
                for i in range(3):
                    row = 16 * (9 * i + 3 * j + k)
                    im_ref[row : row + 16, at] = term[16 * i : 16 * i + 16]


def kernel(
    factor,
    x_hbm, g_hbm, w1_hbm, w2_hbm,
    cells_hbm, grads_hbm,
    x_ref, g_ref, w1, w2,
    ga, gb, z1, z2, r1, r2, f1, f2, y_ref, p_ref, hm1, hp1, rhm1, rhp1, hm2, hp2, rhm2, rhp2,
    xm, xp, rxm, rxp, am, ap, ram, rap, imx, ima, gsum, gout, gin2, mine, sent, rr, part, other, full, oc, oall,
    in_sem, out_sem, w_send, w_recv, v_send, v_recv, a_send, a_recv,
    h_send, h_recv, n_send, n_recv, c_send, c_recv, r_send, r_recv, x_send, x_recv, f_send, f_recv, o_send, o_recv,
):
    d = lax.axis_index("dp")
    s = lax.axis_index("space")
    m, e = d // 2, d % 2
    xl, y = m // 4, m % 4
    z, xh = s // 2, s % 2
    above = lax.rem(s + 1, 16)
    below = lax.rem(s + 15, 16)
    first, final = s == 0, s == 15
    sibling = 2 * m + 1 - e
    across = 2 * z + 1 - xh
    up, down, far = [lax.rem(y + step, 4) for step in (1, 3, 2)]
    side = (1 - xl) * 4
    U, D, O, X = xl * 4 + up, xl * 4 + down, xl * 4 + far, side + y
    XU, XD, XO = side + up, side + down, side + far
    channels = pl.ds(pl.multiple_of(m * 32, 32), 32)

    def rows_of(index, count):
        return pl.ds(pl.multiple_of(index * count, count), count)

    def remote(src, dst, send, recv, dp, space):
        return pltpu.make_async_remote_copy(
            src_ref=src, dst_ref=dst, send_sem=send, recv_sem=recv, device_id=(dp, space), device_id_type=MESH
        )

    def each(count, body, start=0):
        def step(i, carry):
            body(i)
            return carry

        lax.fori_loop(start, count, step, 0)

    barrier = pltpu.get_barrier_semaphore()

    def greet(dp, space):
        pl.semaphore_signal(barrier, inc=1, device_id=(dp, space), device_id_type=MESH)

    each(8, lambda r: greet(2 * lax.rem(m + r, 8) + e, s), 1)
    each(8, lambda r: greet(d, 2 * lax.rem(z + r, 8) + xh), 1)
    greet(sibling, s)
    greet(d, above)
    greet(d, below)
    each(4, lambda r: greet(2 * (side + r) + e, across))

    pairs = [(x_hbm, x_ref), (g_hbm, g_ref), (w1_hbm, w1.at[e]), (w2_hbm, w2.at[e])]
    loads = [pltpu.make_async_copy(src, dst, in_sem.at[i]) for i, (src, dst) in enumerate(pairs)]
    for load in loads:
        load.start()

    def block(phase, t, chip):
        if phase == 0:
            return ga.at[chip // 2, t, :, pl.ds(pl.multiple_of(lax.rem(chip, 2) * 128, 128), 128)]
        return gb.at[t, :, rows_of(chip, 32), :]

    HOPS = [
        (m, None, X, X), (m, None, U, D), (m, None, D, U), (X, None, U, XD), (X, None, D, XU),
        (D, 0, U, O), (U, 1, D, O), (XD, 0, U, XO), (XU, 1, D, XO),
    ]

    def hop(phase, t, kind, arriving=False):
        chip, half, to, source = HOPS[kind]
        ref = block(phase, t, source if arriving else chip)
        if half is not None:
            ref = ref.at[pl.ds(128 * half, 128)] if phase == 0 else ref.at[pl.ds(2 * half, 2)]
        return remote(ref, ref, a_send.at[phase, t, kind], a_recv.at[phase, t, kind], 2 * to + e, s)

    def landed(phase, t, *kinds):
        for kind in kinds:
            hop(phase, t, kind, True).wait_recv()

    def depart(phase, t):
        for kind in range(3):
            hop(phase, t, kind).start()

    def relay(phase, t):
        for kind, then in ((0, (3, 4)), (1, (5,)), (2, (6,))):
            landed(phase, t, kind)
            for more in then:
                hop(phase, t, more).start()

    def relay_more(phase, t):
        for kind, more in ((3, 7), (4, 8)):
            landed(phase, t, kind)
            hop(phase, t, more).start()

    def slices(which, src, r, to, source):
        space = jnp.where(to // 4 == xl, s, across)
        return remote(
            src.at[pl.ds(2 * to, 2)], r.at[:, source, e],
            w_send.at[which, to], w_recv.at[which, source], 2 * to + e, space,
        )

    def cores(index, src, dst):
        return remote(src, dst, v_send.at[index], v_recv.at[index], sibling, s)

    def send_slices(which, src, r):
        each(8, lambda step: slices(which, src, r, lax.rem(m + step, 8), m).start(), 1)
        for slot in range(2):
            r[slot, m, e] = src[2 * m + slot]

    def pass_slices(which, src, r):
        def body(step):
            at = lax.rem(m + 8 - step, 8)
            slices(which, src, r, at, at).wait_recv()

        each(8, body, 1)
        cores(which, r.at[:, :, e], r.at[:, :, e]).start()

    def wait_slices(which, r, f):
        cores(which, r.at[:, :, 1 - e], r.at[:, :, 1 - e]).wait_recv()
        for slot in range(2):
            f[slot] = r[slot].reshape(C, 512).astype(F32).T.astype(BF16)

    mine_at = pl.ds(pl.multiple_of(lax.rem(m, 2) * 128, 128), 128)
    loads[0].wait()
    ga[m // 2, 0, :, mine_at] = x_ref[...].astype(F32).T.astype(BF16)
    loads[1].wait()
    ga[m // 2, 1, :, mine_at] = g_ref[...].astype(F32).T.astype(BF16)
    loads[2].wait()
    regroup(w1.at[e], z1)
    loads[3].wait()
    regroup(w2.at[e], z2)
    sent[:, TILES:] = jnp.zeros((2, 8 * SHARE - TILES, 16, 128), BF16)
    mine[:, TILES:] = jnp.zeros((2, 8 * SHARE - TILES, 16, 128), F32)
    pl.semaphore_wait(barrier, 21)

    depart(0, 0)
    send_slices(0, z1, r1)
    depart(0, 1)
    cores(2, w2.at[e], w2.at[e]).start()
    relay(0, 0)
    pass_slices(0, z1, r1)
    relay(0, 1)
    relay_more(0, 0)
    wait_slices(0, r1, f1)
    cores(2, w2.at[1 - e], w2.at[1 - e]).wait_recv()

    hm, hp, rhm, rhp = (hm1, hm2), (hp1, hp2), (rhm1, rhm2), (rhp1, rhp2)

    def halo_copies(phase, pair):
        return (
            remote(hm[phase].at[pair], rhm[phase].at[pair], h_send.at[phase, 0, pair], h_recv.at[phase, 0, pair], d, below),
            remote(hp[phase].at[pair], rhp[phase].at[pair], h_send.at[phase, 1, pair], h_recv.at[phase, 1, pair], d, above),
        )

    own_pair, other_pair = xl * 2 + y // 2, xl * 2 + 1 - y // 2
    ORDER = [own_pair, other_pair, side // 2 + y // 2, side // 2 + 1 - y // 2]

    def pair_at(i):
        pair = ORDER[0]
        for at in range(1, 4):
            pair = jnp.where(i == at, ORDER[at], pair)
        return pair

    def convolve(phase, pair, f, v, w, g):
        for slot in range(2):
            rows = pl.ds(16 * slot, 16)
            for t in range(2):
                y = y_ref.at[2 * slot + t]
                y[...] = dot(f[slot, :ROWS], v()) if t == 0 else dot(w[slot], g())
                gather_taps(
                    y, p_ref.at[t, pair, rows], hm[phase].at[pair, t, rows], hp[phase].at[pair, t, rows], 1 - 2 * t
                )
        for copy in halo_copies(phase, pair):
            copy.start()

    def phase_one(i):
        for at, kinds in ((1, (5, 6)), (3, (7, 8))):
            @pl.when(i == at)
            def _():
                if at == 1:
                    relay_more(0, 1)
                for t in range(2):
                    landed(0, t, *kinds)

        pair = pair_at(i)
        convolve(0, pair, f1, lambda: ga[pair, 0], w2, lambda: ga[pair, 1])

    each(4, phase_one)
    cores(3, w1.at[e], w1.at[e]).start()
    send_slices(1, z2, r2)

    def near(index, src, dst, to):
        return remote(src, dst, n_send.at[index], n_recv.at[index], d, to)

    def x_edges(pair):
        lowest, highest = edge_planes(ga[pair, 0, channels, :].astype(F32))
        xm[pair] = lowest.astype(BF16)
        xp[pair] = highest.astype(BF16)

    each(4, x_edges)

    def halo_of(phase, t, pair):
        return jnp.concatenate(spread_halo(rhp[phase][pair, t], rhm[phase][pair, t], first, final), axis=1)

    def middle(i):
        pair = pair_at(i)
        for copy in halo_copies(0, pair):
            copy.wait_recv()
        pre = p_ref[0, pair] + halo_of(0, 0, pair)
        grad = p_ref[1, pair] + halo_of(0, 1, pair)
        sig = jax.nn.sigmoid(pre)
        act = (pre * sig).astype(BF16)
        gb[0, pair, channels, :] = act
        gb[1, pair, channels, :] = (grad * sig * (1.0 + pre * (1.0 - sig))).astype(BF16)
        lowest, highest = edge_planes(act.astype(F32))
        am[pair] = lowest.astype(BF16)
        ap[pair] = highest.astype(BF16)

    each(4, middle)
    depart(1, 1)
    near(2, am, ram, below).start()
    near(3, ap, rap, above).start()
    depart(1, 0)
    near(0, xm, rxm, below).start()
    near(1, xp, rxp, above).start()

    def taps(pair, v, up_halo, down_halo, im):
        for slot in range(2):
            rows = slice(16 * slot, 16 * slot + 16)
            halos = spread_halo(up_halo[pair, rows], down_halo[pair, rows], first, final)
            scatter_taps(v[rows], halos, im.at[pair, slot])

    def taps_x(pair):
        taps(pair, ga[pair, 0, channels, :].astype(F32), rxp, rxm, imx)

    def taps_a(pair):
        taps(pair, gb[0, pair, channels, :].astype(F32), rap, ram, ima)

    def core_copy(which):
        return remote(gout.at[which], gin2.at[which], c_send.at[which], c_recv.at[which], sibling, s)

    def reduce_copy(which, step):
        to = lax.rem(z + step, 8)
        return remote(
            sent.at[which, pl.ds(to * SHARE, SHARE)], rr.at[which, step],
            r_send.at[which, step], r_recv.at[which, step], d, 2 * to + xh,
        )

    def product(im, slot, operand, total):
        total[...] = dot(im[0, slot], operand(0), ((1,), (1,)))

        def add(pair):
            total[...] += dot(im[pair, slot], operand(pair), ((1,), (1,)))

        each(4, add, 1)

    def send_partial(which, im, operand):
        product(im, 1 - e, operand, gout.at[which])
        core_copy(which).start()
        product(im, e, operand, gsum)
        core_copy(which).wait_recv()
        for tile in range(TILES):
            row, lane = tile // 2 * 16, tile % 2 * 128
            at = (slice(row, row + 16), slice(lane, lane + 128))
            value = gsum[at] + gin2[(which, *at)]
            mine[which, tile] = value
            sent[which, tile] = value.astype(BF16)
        for step in (4, 3, 5, 2, 6, 1, 7):
            reduce_copy(which, step).start()

    def pair_copy(which):
        return remote(part.at[which], other.at[which], x_send.at[which], x_recv.at[which], d, 2 * z + 1 - xh)

    def reduce_ring(which):
        each(8, lambda step: reduce_copy(which, step).wait_recv(), 1)
        total = mine[which, pl.ds(z * SHARE, SHARE)]
        for step in range(1, 8):
            total += rr[which, step].astype(F32)
        part[which] = total
        pair_copy(which).start()

    CUT = SHARE // 2 + 1
    STEPS = [
        (0, 0, SHARE, 2), (0, 0, SHARE, -2),
        (-2, 0, SHARE, -1), (-2, 0, SHARE, 1), (2, 0, SHARE, 1), (2, 0, SHARE, -1),
        (-2, 0, CUT, 2), (2, CUT, SHARE, -2),
    ]

    def spread_copy(which, kind, arriving=False):
        owner, low, high, far_to = STEPS[kind]
        if arriving:
            owner = owner - far_to
        ref = full.at[which, pl.ds(lax.rem(z + owner + 8, 8) * SHARE + low, high - low)]
        to = 2 * lax.rem(z + far_to + 8, 8) + xh
        return remote(ref, ref, f_send.at[which, kind], f_recv.at[which, kind], d, to)

    def spread(which):
        pair_copy(which).wait_recv()
        full[which, pl.ds(z * SHARE, SHARE)] = ((part[which] + other[which]) * factor).astype(BF16)
        spread_copy(which, 0).start()
        spread_copy(which, 1).start()

    def spread_on(which):
        for kind, then in ((0, (6, 3, 2)), (1, (7, 5, 4))):
            spread_copy(which, kind, True).wait_recv()
            for more in then:
                spread_copy(which, more).start()

    def result(which):
        src, dst = (oall, cells_hbm) if which == 2 else (full.at[which], grads_hbm.at[which])
        return pltpu.make_async_copy(src, dst, out_sem.at[which])

    def spread_end(which):
        for kind in range(2, 8):
            spread_copy(which, kind, True).wait_recv()
        result(which).start()

    relay(1, 1)
    near(2, am, ram, below).wait_recv()
    near(3, ap, rap, above).wait_recv()
    each(4, taps_a)
    relay(1, 0)
    relay_more(1, 1)
    send_partial(1, ima, lambda pair: ga[pair, 1])
    near(0, xm, rxm, below).wait_recv()
    near(1, xp, rxp, above).wait_recv()
    each(4, taps_x)
    relay_more(1, 0)
    landed(1, 1, 5, 6, 7, 8)
    send_partial(0, imx, lambda pair: gb[1, pair])
    pass_slices(1, z2, r2)
    landed(1, 0, 5, 6, 7, 8)
    wait_slices(1, r2, f2)
    cores(3, w1.at[1 - e], w1.at[1 - e]).wait_recv()

    def phase_two(i):
        @pl.when(i == 2)
        def _():
            reduce_ring(1)

        pair = pair_at(i)
        convolve(1, pair, f2, lambda: gb[0, pair], w1, lambda: gb[1, pair])

    each(4, phase_two)
    reduce_ring(0)
    spread(1)

    def home(to, source):
        return remote(oc.at[to], oall.at[source], o_send.at[to], o_recv.at[source], 2 * to + e, s)

    def finish(i):
        pair = pair_at(i)
        for copy in halo_copies(1, pair):
            copy.wait_recv()
        for t in range(2):
            total = p_ref[t, pair] + halo_of(1, t, pair)
            total = (ga[pair, t, channels, :].astype(F32) + total).astype(BF16)
            oc[2 * pair, t] = total[:, :128]
            oc[2 * pair + 1, t] = total[:, 128:]
        for half in range(2):
            to = 2 * pair + half

            @pl.when(to != m)
            def _():
                home(to, m).start()

    each(4, finish)
    spread(0)
    spread_on(1)
    oall[m] = oc[m]

    def wait_home(step):
        source = lax.rem(m + 8 - step, 8)
        home(source, source).wait_recv()

    each(8, wait_home, 1)
    result(2).start()
    spread_on(0)
    spread_end(1)
    spread_end(0)
    for which in range(3):
        result(which).wait()

    def wait_far(step):
        to = lax.rem(m + step, 8)
        home(to, m).wait_send()
        slices(0, z1, r1, to, m).wait_send()
        slices(1, z2, r2, to, m).wait_send()
        for which in range(2):
            reduce_copy(which, step).wait_send()

    each(8, wait_far, 1)

    def wait_halo(pair):
        for phase in range(2):
            for copy in halo_copies(phase, pair):
                copy.wait_send()

    each(4, wait_halo)
    cores(0, r1.at[:, :, e], r1.at[:, :, e]).wait_send()
    cores(1, r2.at[:, :, e], r2.at[:, :, e]).wait_send()
    cores(2, w2.at[e], w2.at[e]).wait_send()
    cores(3, w1.at[e], w1.at[e]).wait_send()
    for t in range(2):
        core_copy(t).wait_send()
        pair_copy(t).wait_send()
        for kind in range(8):
            spread_copy(t, kind).wait_send()
        for phase in range(2):
            for kind in range(9):
                hop(phase, t, kind).wait_send()
    near(0, xm, rxm, below).wait_send()
    near(1, xp, rxp, above).wait_send()
    near(2, am, ram, below).wait_send()
    near(3, ap, rap, above).wait_send()


def lay_out(cells_ref, grads_ref, out_ref, gin_ref, one_ref, two_ref):
    for t, ref in enumerate((out_ref, gin_ref)):
        ref[...] = cells_ref[:, t].reshape(C, 128).astype(F32).T.astype(BF16)
    for which, ref in enumerate((one_ref, two_ref)):
        for tile in range(TILES):
            row, lane = tile // 2 * 16, tile % 2 * 128
            ref[row : row + 16, lane : lane + 128] = grads_ref[which, tile].astype(F32)


def shards(features, weight_one, weight_two, cotangent):
    shape = features.shape
    count = shape[0] * lax.axis_size("dp") * shape[1] * lax.axis_size("space") * shape[2] * shape[3]
    factor = float(count) ** (-0.5)
    vmem = pl.BlockSpec(memory_space=pltpu.VMEM)
    dma = pltpu.SemaphoreType.DMA
    scratch = pltpu.VMEM
    cells, grads = pl.pallas_call(
        functools.partial(kernel, factor),
        out_shape=[
            jax.ShapeDtypeStruct((8, 2, 32, 128), BF16),
            jax.ShapeDtypeStruct((2, 8 * SHARE, 16, 128), BF16),
        ],
        in_specs=[pl.BlockSpec(memory_space=pl.ANY)] * 4,
        out_specs=[pl.BlockSpec(memory_space=pl.ANY)] * 2,
        scratch_shapes=[
            scratch((128, C), BF16), scratch((128, C), BF16),
            scratch((2, ROWS, C), BF16), scratch((2, ROWS, C), BF16),
            scratch((4, 2, C, C), BF16),
            scratch((2, 4, C, C), BF16),
            scratch((16, 16, 512), BF16), scratch((16, 16, 512), BF16),
            scratch((2, 8, 2, 16, 512), BF16), scratch((2, 8, 2, 16, 512), BF16),
            scratch((2, 512, C), BF16), scratch((2, 512, C), BF16),
            scratch((4, ROWS, C), F32),
            scratch((2, 4, 32, C), F32),
            *[scratch((4, 2, 32, 128), F32)] * 4,
            *[scratch((4, 2, 32, 128), BF16)] * 4,
            *[scratch((4, 32, 128), BF16)] * 8,
            scratch((4, 2, ROWS, C), BF16), scratch((4, 2, ROWS, C), BF16),
            scratch((ROWS, C), F32),
            scratch((2, ROWS, C), F32), scratch((2, ROWS, C), F32),
            scratch((2, 8 * SHARE, 16, 128), F32),
            scratch((2, 8 * SHARE, 16, 128), BF16),
            scratch((2, 8, SHARE, 16, 128), BF16),
            scratch((2, SHARE, 16, 128), F32), scratch((2, SHARE, 16, 128), F32),
            scratch((2, 8 * SHARE, 16, 128), BF16),
            scratch((8, 2, 32, 128), BF16), scratch((8, 2, 32, 128), BF16),
            dma((4,)), dma((3,)),
            dma((2, 8)), dma((2, 8)), dma((4,)), dma((4,)),
            dma((2, 2, 9)), dma((2, 2, 9)),
            dma((2, 2, 4)), dma((2, 2, 4)),
            dma((4,)), dma((4,)), dma((2,)), dma((2,)),
            dma((2, 8)), dma((2, 8)), dma((2,)), dma((2,)), dma((2, 8)), dma((2, 8)),
            dma((8,)), dma((8,)),
        ],
        compiler_params=pltpu.CompilerParams(
            collective_id=0, has_side_effects=True, vmem_limit_bytes=56 * 2**20
        ),
    )(
        features.reshape(128, C), cotangent.reshape(128, C),
        weight_one.reshape(ROWS, C), weight_two.reshape(ROWS, C),
    )
    out, gin, one, two = pl.pallas_call(
        lay_out,
        out_shape=[
            jax.ShapeDtypeStruct((128, C), BF16),
            jax.ShapeDtypeStruct((128, C), BF16),
            jax.ShapeDtypeStruct((ROWS, C), F32),
            jax.ShapeDtypeStruct((ROWS, C), F32),
        ],
        in_specs=[vmem] * 2,
        out_specs=[vmem] * 4,
    )(cells, grads)
    return out.reshape(shape), gin.reshape(shape), one.reshape(TAPS, 16, C), two.reshape(TAPS, 16, C)


def solution(mesh):
    in_specs = (
        P("dp", "space", None, None, None),
        P(None, "dp", None),
        P(None, "dp", None),
        P("dp", "space", None, None, None),
    )
    out_specs = (
        P("dp", "space", None, None, None),
        P("dp", "space", None, None, None),
        P(None, "dp", None),
        P(None, "dp", None),
    )
    return jax.shard_map(shards, mesh=mesh, in_specs=in_specs, out_specs=out_specs, check_vma=False)
```

```python
import functools

import jax
import jax.numpy as jnp
from jax import lax
from jax.experimental import pallas as pl
from jax.experimental.pallas import tpu as pltpu
from jax.sharding import PartitionSpec as P

MESH = pl.DeviceIdType.MESH
F32 = jnp.float32
BF16 = jnp.bfloat16
C = 256
TAPS = 27
ROWS = TAPS * 16
TILES = 2 * TAPS
SHARE = -(-TILES // 8)


def dot(a, b, dims=((1,), (0,))):
    return lax.dot_general(a, b, (dims, ((), ())), preferred_element_type=F32)


def lanes():
    return lax.broadcasted_iota(jnp.int32, (16, 128), 1)


def lower(rows=16):
    return lax.broadcasted_iota(jnp.int32, (rows, 128), 1) < 64


def half_turn(v):
    return pltpu.roll(v, 64, 1)


def inside(j, k, sign):
    lane = lanes()
    y = (lane // 8) % 8 + sign * (j - 1)
    z = lane % 8 + sign * (k - 1)
    return (y >= 0) & (y < 8) & (z >= 0) & (z < 8)


def shifted(v, j, k, sign):
    delta = sign * (8 * (j - 1) + (k - 1))
    if delta == 0:
        return v
    parts = v.shape[0] // 16
    keep = inside(j, k, sign)
    if parts > 1:
        keep = jnp.concatenate([keep] * parts, axis=0)
    return jnp.where(keep, pltpu.roll(v, (-delta) % 128, 1), 0.0)


def regroup(w_ref, z_ref):
    group = lanes() // 16
    for q in range(4):
        for h in range(2):
            tiles = []
            for i in range(8):
                tap = 8 * q + i
                if tap < TAPS:
                    tiles.append(w_ref[16 * tap : 16 * tap + 16, 128 * h : 128 * h + 128].astype(F32))
                else:
                    tiles.append(jnp.zeros((16, 128), F32))
            for bit in (1, 2, 4):
                low = (group & bit) == 0
                for i in range(8):
                    if i & bit:
                        continue
                    a, b = tiles[i], tiles[i + bit]
                    tiles[i] = jnp.where(low, a, pltpu.roll(b, 16 * bit, 1))
                    tiles[i + bit] = jnp.where(low, pltpu.roll(a, 128 - 16 * bit, 1), b)
            for i in range(8):
                z_ref[8 * h + i, :, 128 * q : 128 * q + 128] = tiles[i].astype(BF16)


def gather_taps(y_ref, p_ref, hm_ref, hp_ref, sign):
    lo = lower()
    lefts = []
    for half in range(2):
        at = slice(128 * half, 128 * half + 128)
        total = None
        for j in range(3):
            for k in range(3):
                rows = [16 * (9 * i + 3 * j + k) for i in range(3)]
                first, mid, last = [y_ref[r : r + 16, at] for r in rows]
                if sign < 0:
                    first, last = last, first
                inner = jnp.where(lo, first, last)
                outer = jnp.where(lo, last, first)
                term = shifted(jnp.concatenate([mid, inner, outer], axis=0), j, k, sign)
                total = term if total is None else total + term
        p_ref[:, at] = total[:16] + half_turn(total[16:32])
        lefts.append(total[32:])
    hm_ref[...] = jnp.where(lo, lefts[0], half_turn(lefts[1])).astype(hm_ref.dtype)
    hp_ref[...] = jnp.where(lo, half_turn(lefts[0]), lefts[1]).astype(hp_ref.dtype)


def spread_halo(hp, hm, first, final):
    lo = lower(hp.shape[0])
    hp = jnp.where(first, 0.0, hp.astype(F32))
    hm = jnp.where(final, 0.0, hm.astype(F32))
    return [jnp.where(lo, hp, half_turn(hm)), jnp.where(lo, half_turn(hp), hm)]


def edge_planes(v):
    lo = lower(v.shape[0])
    a, b = v[:, :128], v[:, 128:]
    return jnp.where(lo, a, half_turn(b)), jnp.where(lo, half_turn(a), b)


def scatter_taps(v, halos, im_ref):
    lo = lower()
    for half in range(2):
        at = slice(128 * half, 128 * half + 128)
        own = v[:, at]
        turned = half_turn(own)
        stack = jnp.concatenate(
            [jnp.where(lo, halos[half], turned), own, jnp.where(lo, turned, halos[half])], axis=0
        )
        for j in range(3):
            for k in range(3):
                term = shifted(stack, j, k, 1).astype(BF16)
                for i in range(3):
                    row = 16 * (9 * i + 3 * j + k)
                    im_ref[row : row + 16, at] = term[16 * i : 16 * i + 16]


def kernel(
    factor,
    x_hbm, g_hbm, w1_hbm, w2_hbm,
    cells_hbm, grads_hbm,
    x_ref, g_ref, w1, w2,
    ga, gb, z1, z2, r1, r2, f1, f2, y_ref, p_ref, hm1, hp1, rhm1, rhp1, hm2, hp2, rhm2, rhp2,
    xm, xp, rxm, rxp, am, ap, ram, rap, imx, ima, gsum, gout, gin2, mine, sent, rr, part, other, full, oc, oall,
    in_sem, out_sem, w_send, w_recv, v_send, v_recv, a_send, a_recv,
    h_send, h_recv, n_send, n_recv, c_send, c_recv, r_send, r_recv, x_send, x_recv, f_send, f_recv, o_send, o_recv,
):
    d = lax.axis_index("dp")
    s = lax.axis_index("space")
    m, e = d // 2, d % 2
    xl, y = m // 4, m % 4
    z, xh = s // 2, s % 2
    above = lax.rem(s + 1, 16)
    below = lax.rem(s + 15, 16)
    first, final = s == 0, s == 15
    sibling = 2 * m + 1 - e
    across = 2 * z + 1 - xh
    up, down, far = [lax.rem(y + step, 4) for step in (1, 3, 2)]
    side = (1 - xl) * 4
    U, D, O, X = xl * 4 + up, xl * 4 + down, xl * 4 + far, side + y
    XU, XD, XO = side + up, side + down, side + far
    channels = pl.ds(pl.multiple_of(m * 32, 32), 32)

    def rows_of(index, count):
        return pl.ds(pl.multiple_of(index * count, count), count)

    def remote(src, dst, send, recv, dp, space):
        return pltpu.make_async_remote_copy(
            src_ref=src, dst_ref=dst, send_sem=send, recv_sem=recv, device_id=(dp, space), device_id_type=MESH
        )

    def each(count, body, start=0):
        def step(i, carry):
            body(i)
            return carry

        lax.fori_loop(start, count, step, 0)

    barrier = pltpu.get_barrier_semaphore()

    def greet(dp, space):
        pl.semaphore_signal(barrier, inc=1, device_id=(dp, space), device_id_type=MESH)

    each(8, lambda r: greet(2 * lax.rem(m + r, 8) + e, s), 1)
    each(8, lambda r: greet(d, 2 * lax.rem(z + r, 8) + xh), 1)
    greet(sibling, s)
    greet(d, above)
    greet(d, below)
    each(4, lambda r: greet(2 * (side + r) + e, across))

    pairs = [(x_hbm, x_ref), (g_hbm, g_ref), (w1_hbm, w1.at[e]), (w2_hbm, w2.at[e])]
    loads = [pltpu.make_async_copy(src, dst, in_sem.at[i]) for i, (src, dst) in enumerate(pairs)]
    for load in loads:
        load.start()

    def block(phase, t, chip):
        if phase == 0:
            return ga.at[chip // 2, t, :, pl.ds(pl.multiple_of(lax.rem(chip, 2) * 128, 128), 128)]
        return gb.at[t, :, rows_of(chip, 32), :]

    HOPS = [
        (m, None, X, X), (m, None, U, D), (m, None, D, U), (X, None, U, XD), (X, None, D, XU),
        (D, 0, U, O), (U, 1, D, O), (XD, 0, U, XO), (XU, 1, D, XO),
    ]

    def hop(phase, t, kind, arriving=False):
        chip, half, to, source = HOPS[kind]
        ref = block(phase, t, source if arriving else chip)
        if half is not None:
            ref = ref.at[pl.ds(128 * half, 128)] if phase == 0 else ref.at[pl.ds(2 * half, 2)]
        return remote(ref, ref, a_send.at[phase, t, kind], a_recv.at[phase, t, kind], 2 * to + e, s)

    def landed(phase, t, *kinds):
        for kind in kinds:
            hop(phase, t, kind, True).wait_recv()

    def depart(phase, t):
        for kind in range(3):
            hop(phase, t, kind).start()

    def relay(phase, t):
        for kind, then in ((0, (3, 4)), (1, (5,)), (2, (6,))):
            landed(phase, t, kind)
            for more in then:
                hop(phase, t, more).start()

    def relay_more(phase, t):
        for kind, more in ((3, 7), (4, 8)):
            landed(phase, t, kind)
            hop(phase, t, more).start()

    def slices(which, src, r, to, source):
        space = jnp.where(to // 4 == xl, s, across)
        return remote(
            src.at[pl.ds(2 * to, 2)], r.at[:, source, e],
            w_send.at[which, to], w_recv.at[which, source], 2 * to + e, space,
        )

    def cores(index, src, dst):
        return remote(src, dst, v_send.at[index], v_recv.at[index], sibling, s)

    def send_slices(which, src, r):
        for to in (XO, O, XU, XD, X, U, D):
            slices(which, src, r, to, m).start()
        for slot in range(2):
            r[slot, m, e] = src[2 * m + slot]

    def pass_slices(which, src, r):
        def body(step):
            at = lax.rem(m + 8 - step, 8)
            slices(which, src, r, at, at).wait_recv()

        each(8, body, 1)
        cores(which, r.at[:, :, e], r.at[:, :, e]).start()

    def wait_slices(which, r, f):
        cores(which, r.at[:, :, 1 - e], r.at[:, :, 1 - e]).wait_recv()
        for slot in range(2):
            f[slot] = r[slot].reshape(C, 512).astype(F32).T.astype(BF16)

    mine_at = pl.ds(pl.multiple_of(lax.rem(m, 2) * 128, 128), 128)
    loads[0].wait()
    ga[m // 2, 0, :, mine_at] = x_ref[...].astype(F32).T.astype(BF16)
    loads[1].wait()
    ga[m // 2, 1, :, mine_at] = g_ref[...].astype(F32).T.astype(BF16)
    loads[2].wait()
    regroup(w1.at[e], z1)
    loads[3].wait()
    regroup(w2.at[e], z2)
    sent[:, TILES:] = jnp.zeros((2, 8 * SHARE - TILES, 16, 128), BF16)
    mine[:, TILES:] = jnp.zeros((2, 8 * SHARE - TILES, 16, 128), F32)
    pl.semaphore_wait(barrier, 21)

    depart(0, 0)
    send_slices(0, z1, r1)
    depart(0, 1)
    cores(2, w2.at[e], w2.at[e]).start()
    relay(0, 0)
    pass_slices(0, z1, r1)
    relay(0, 1)
    relay_more(0, 0)
    wait_slices(0, r1, f1)
    cores(2, w2.at[1 - e], w2.at[1 - e]).wait_recv()

    hm, hp, rhm, rhp = (hm1, hm2), (hp1, hp2), (rhm1, rhm2), (rhp1, rhp2)

    def halo_copies(phase, pair):
        return (
            remote(hm[phase].at[pair], rhm[phase].at[pair], h_send.at[phase, 0, pair], h_recv.at[phase, 0, pair], d, below),
            remote(hp[phase].at[pair], rhp[phase].at[pair], h_send.at[phase, 1, pair], h_recv.at[phase, 1, pair], d, above),
        )

    own_pair, other_pair = xl * 2 + y // 2, xl * 2 + 1 - y // 2
    ORDER = [own_pair, other_pair, side // 2 + y // 2, side // 2 + 1 - y // 2]

    def pair_at(i):
        pair = ORDER[0]
        for at in range(1, 4):
            pair = jnp.where(i == at, ORDER[at], pair)
        return pair

    def convolve(phase, pair, f, v, w, g):
        for slot in range(2):
            rows = pl.ds(16 * slot, 16)
            for t in range(2):
                y = y_ref.at[2 * slot + t]
                y[...] = dot(f[slot, :ROWS], v()) if t == 0 else dot(w[slot], g())
                gather_taps(
                    y, p_ref.at[t, pair, rows], hm[phase].at[pair, t, rows], hp[phase].at[pair, t, rows], 1 - 2 * t
                )
        for copy in halo_copies(phase, pair):
            copy.start()

    def phase_one(i):
        for at, kinds in ((1, (5, 6)), (3, (7, 8))):
            @pl.when(i == at)
            def _():
                if at == 1:
                    relay_more(0, 1)
                for t in range(2):
                    landed(0, t, *kinds)

        pair = pair_at(i)
        convolve(0, pair, f1, lambda: ga[pair, 0], w2, lambda: ga[pair, 1])

    each(4, phase_one)
    cores(3, w1.at[e], w1.at[e]).start()
    send_slices(1, z2, r2)

    def near(index, src, dst, to):
        return remote(src, dst, n_send.at[index], n_recv.at[index], d, to)

    def x_edges(pair):
        lowest, highest = edge_planes(ga[pair, 0, channels, :].astype(F32))
        xm[pair] = lowest.astype(BF16)
        xp[pair] = highest.astype(BF16)

    each(4, x_edges)

    def halo_of(phase, t, pair):
        return jnp.concatenate(spread_halo(rhp[phase][pair, t], rhm[phase][pair, t], first, final), axis=1)

    def middle(i):
        pair = pair_at(i)
        for copy in halo_copies(0, pair):
            copy.wait_recv()
        pre = p_ref[0, pair] + halo_of(0, 0, pair)
        grad = p_ref[1, pair] + halo_of(0, 1, pair)
        sig = jax.nn.sigmoid(pre)
        act = (pre * sig).astype(BF16)
        gb[0, pair, channels, :] = act
        gb[1, pair, channels, :] = (grad * sig * (1.0 + pre * (1.0 - sig))).astype(BF16)
        lowest, highest = edge_planes(act.astype(F32))
        am[pair] = lowest.astype(BF16)
        ap[pair] = highest.astype(BF16)

    each(4, middle)
    depart(1, 1)
    near(2, am, ram, below).start()
    near(3, ap, rap, above).start()
    depart(1, 0)
    near(0, xm, rxm, below).start()
    near(1, xp, rxp, above).start()

    def taps(pair, v, up_halo, down_halo, im):
        for slot in range(2):
            rows = slice(16 * slot, 16 * slot + 16)
            halos = spread_halo(up_halo[pair, rows], down_halo[pair, rows], first, final)
            scatter_taps(v[rows], halos, im.at[pair, slot])

    def taps_x(pair):
        taps(pair, ga[pair, 0, channels, :].astype(F32), rxp, rxm, imx)

    def taps_a(pair):
        taps(pair, gb[0, pair, channels, :].astype(F32), rap, ram, ima)

    def core_copy(which):
        return remote(gout.at[which], gin2.at[which], c_send.at[which], c_recv.at[which], sibling, s)

    def reduce_copy(which, step):
        to = lax.rem(z + step, 8)
        return remote(
            sent.at[which, pl.ds(to * SHARE, SHARE)], rr.at[which, step],
            r_send.at[which, step], r_recv.at[which, step], d, 2 * to + xh,
        )

    def product(im, slot, operand, total):
        total[...] = dot(im[0, slot], operand(0), ((1,), (1,)))

        def add(pair):
            total[...] += dot(im[pair, slot], operand(pair), ((1,), (1,)))

        each(4, add, 1)

    def send_partial(which, im, operand):
        product(im, 1 - e, operand, gout.at[which])
        core_copy(which).start()
        product(im, e, operand, gsum)
        core_copy(which).wait_recv()
        for tile in range(TILES):
            row, lane = tile // 2 * 16, tile % 2 * 128
            at = (slice(row, row + 16), slice(lane, lane + 128))
            value = gsum[at] + gin2[(which, *at)]
            mine[which, tile] = value
            sent[which, tile] = value.astype(BF16)
        for step in (4, 3, 5, 2, 6, 1, 7):
            reduce_copy(which, step).start()

    def pair_copy(which):
        return remote(part.at[which], other.at[which], x_send.at[which], x_recv.at[which], d, 2 * z + 1 - xh)

    def reduce_ring(which):
        each(8, lambda step: reduce_copy(which, step).wait_recv(), 1)
        total = mine[which, pl.ds(z * SHARE, SHARE)]
        for step in range(1, 8):
            total += rr[which, step].astype(F32)
        part[which] = total
        pair_copy(which).start()

    CUT = SHARE // 2 + 1
    STEPS = [
        (0, 0, SHARE, 2), (0, 0, SHARE, -2),
        (-2, 0, SHARE, -1), (-2, 0, SHARE, 1), (2, 0, SHARE, 1), (2, 0, SHARE, -1),
        (-2, 0, CUT, 2), (2, CUT, SHARE, -2),
    ]

    def spread_copy(which, kind, arriving=False):
        owner, low, high, far_to = STEPS[kind]
        if arriving:
            owner = owner - far_to
        ref = full.at[which, pl.ds(lax.rem(z + owner + 8, 8) * SHARE + low, high - low)]
        to = 2 * lax.rem(z + far_to + 8, 8) + xh
        return remote(ref, ref, f_send.at[which, kind], f_recv.at[which, kind], d, to)

    def spread(which):
        pair_copy(which).wait_recv()
        full[which, pl.ds(z * SHARE, SHARE)] = ((part[which] + other[which]) * factor).astype(BF16)
        spread_copy(which, 0).start()
        spread_copy(which, 1).start()

    def spread_on(which):
        for kind, then in ((0, (6, 3, 2)), (1, (7, 5, 4))):
            spread_copy(which, kind, True).wait_recv()
            for more in then:
                spread_copy(which, more).start()

    def result(which):
        src, dst = (oall, cells_hbm) if which == 2 else (full.at[which], grads_hbm.at[which])
        return pltpu.make_async_copy(src, dst, out_sem.at[which])

    def spread_end(which):
        for kind in range(2, 8):
            spread_copy(which, kind, True).wait_recv()
        result(which).start()

    relay(1, 1)
    near(2, am, ram, below).wait_recv()
    near(3, ap, rap, above).wait_recv()
    each(4, taps_a)
    relay(1, 0)
    relay_more(1, 1)
    send_partial(1, ima, lambda pair: ga[pair, 1])
    near(0, xm, rxm, below).wait_recv()
    near(1, xp, rxp, above).wait_recv()
    each(4, taps_x)
    relay_more(1, 0)
    landed(1, 1, 5, 6, 7, 8)
    send_partial(0, imx, lambda pair: gb[1, pair])
    pass_slices(1, z2, r2)
    landed(1, 0, 5, 6, 7, 8)
    wait_slices(1, r2, f2)
    cores(3, w1.at[1 - e], w1.at[1 - e]).wait_recv()

    def phase_two(i):
        @pl.when(i == 2)
        def _():
            reduce_ring(1)

        pair = pair_at(3 - i)
        convolve(1, pair, f2, lambda: gb[0, pair], w1, lambda: gb[1, pair])

    each(4, phase_two)
    reduce_ring(0)
    spread(1)

    def home(to, source):
        return remote(oc.at[to], oall.at[source], o_send.at[to], o_recv.at[source], 2 * to + e, s)

    def finish(i):
        pair = pair_at(3 - i)
        for copy in halo_copies(1, pair):
            copy.wait_recv()
        for t in range(2):
            total = p_ref[t, pair] + halo_of(1, t, pair)
            total = (ga[pair, t, channels, :].astype(F32) + total).astype(BF16)
            oc[2 * pair, t] = total[:, :128]
            oc[2 * pair + 1, t] = total[:, 128:]
        for half in range(2):
            to = 2 * pair + half

            @pl.when(to != m)
            def _():
                home(to, m).start()

    each(4, finish)
    spread(0)
    spread_on(1)
    spread_on(0)
    oall[m] = oc[m]

    def wait_home(step):
        source = lax.rem(m + 8 - step, 8)
        home(source, source).wait_recv()

    each(8, wait_home, 1)
    result(2).start()
    spread_end(1)
    spread_end(0)
    for which in range(3):
        result(which).wait()

    def wait_far(step):
        to = lax.rem(m + step, 8)
        home(to, m).wait_send()
        slices(0, z1, r1, to, m).wait_send()
        slices(1, z2, r2, to, m).wait_send()
        for which in range(2):
            reduce_copy(which, step).wait_send()

    each(8, wait_far, 1)

    def wait_halo(pair):
        for phase in range(2):
            for copy in halo_copies(phase, pair):
                copy.wait_send()

    each(4, wait_halo)
    cores(0, r1.at[:, :, e], r1.at[:, :, e]).wait_send()
    cores(1, r2.at[:, :, e], r2.at[:, :, e]).wait_send()
    cores(2, w2.at[e], w2.at[e]).wait_send()
    cores(3, w1.at[e], w1.at[e]).wait_send()
    for t in range(2):
        core_copy(t).wait_send()
        pair_copy(t).wait_send()
        for kind in range(8):
            spread_copy(t, kind).wait_send()
        for phase in range(2):
            for kind in range(9):
                hop(phase, t, kind).wait_send()
    near(0, xm, rxm, below).wait_send()
    near(1, xp, rxp, above).wait_send()
    near(2, am, ram, below).wait_send()
    near(3, ap, rap, above).wait_send()


def lay_out(cells_ref, grads_ref, out_ref, gin_ref, one_ref, two_ref):
    for t, ref in enumerate((out_ref, gin_ref)):
        ref[...] = cells_ref[:, t].reshape(C, 128).astype(F32).T.astype(BF16)
    for which, ref in enumerate((one_ref, two_ref)):
        for tile in range(TILES):
            row, lane = tile // 2 * 16, tile % 2 * 128
            ref[row : row + 16, lane : lane + 128] = grads_ref[which, tile].astype(F32)


def shards(features, weight_one, weight_two, cotangent):
    shape = features.shape
    count = shape[0] * lax.axis_size("dp") * shape[1] * lax.axis_size("space") * shape[2] * shape[3]
    factor = float(count) ** (-0.5)
    vmem = pl.BlockSpec(memory_space=pltpu.VMEM)
    dma = pltpu.SemaphoreType.DMA
    scratch = pltpu.VMEM
    cells, grads = pl.pallas_call(
        functools.partial(kernel, factor),
        out_shape=[
            jax.ShapeDtypeStruct((8, 2, 32, 128), BF16),
            jax.ShapeDtypeStruct((2, 8 * SHARE, 16, 128), BF16),
        ],
        in_specs=[pl.BlockSpec(memory_space=pl.ANY)] * 4,
        out_specs=[pl.BlockSpec(memory_space=pl.ANY)] * 2,
        scratch_shapes=[
            scratch((128, C), BF16), scratch((128, C), BF16),
            scratch((2, ROWS, C), BF16), scratch((2, ROWS, C), BF16),
            scratch((4, 2, C, C), BF16),
            scratch((2, 4, C, C), BF16),
            scratch((16, 16, 512), BF16), scratch((16, 16, 512), BF16),
            scratch((2, 8, 2, 16, 512), BF16), scratch((2, 8, 2, 16, 512), BF16),
            scratch((2, 512, C), BF16), scratch((2, 512, C), BF16),
            scratch((4, ROWS, C), F32),
            scratch((2, 4, 32, C), F32),
            *[scratch((4, 2, 32, 128), F32)] * 4,
            *[scratch((4, 2, 32, 128), BF16)] * 4,
            *[scratch((4, 32, 128), BF16)] * 8,
            scratch((4, 2, ROWS, C), BF16), scratch((4, 2, ROWS, C), BF16),
            scratch((ROWS, C), F32),
            scratch((2, ROWS, C), F32), scratch((2, ROWS, C), F32),
            scratch((2, 8 * SHARE, 16, 128), F32),
            scratch((2, 8 * SHARE, 16, 128), BF16),
            scratch((2, 8, SHARE, 16, 128), BF16),
            scratch((2, SHARE, 16, 128), F32), scratch((2, SHARE, 16, 128), F32),
            scratch((2, 8 * SHARE, 16, 128), BF16),
            scratch((8, 2, 32, 128), BF16), scratch((8, 2, 32, 128), BF16),
            dma((4,)), dma((3,)),
            dma((2, 8)), dma((2, 8)), dma((4,)), dma((4,)),
            dma((2, 2, 9)), dma((2, 2, 9)),
            dma((2, 2, 4)), dma((2, 2, 4)),
            dma((4,)), dma((4,)), dma((2,)), dma((2,)),
            dma((2, 8)), dma((2, 8)), dma((2,)), dma((2,)), dma((2, 8)), dma((2, 8)),
            dma((8,)), dma((8,)),
        ],
        compiler_params=pltpu.CompilerParams(
            collective_id=0, has_side_effects=True, vmem_limit_bytes=56 * 2**20
        ),
    )(
        features.reshape(128, C), cotangent.reshape(128, C),
        weight_one.reshape(ROWS, C), weight_two.reshape(ROWS, C),
    )
    out, gin, one, two = pl.pallas_call(
        lay_out,
        out_shape=[
            jax.ShapeDtypeStruct((128, C), BF16),
            jax.ShapeDtypeStruct((128, C), BF16),
            jax.ShapeDtypeStruct((ROWS, C), F32),
            jax.ShapeDtypeStruct((ROWS, C), F32),
        ],
        in_specs=[vmem] * 2,
        out_specs=[vmem] * 4,
    )(cells, grads)
    return out.reshape(shape), gin.reshape(shape), one.reshape(TAPS, 16, C), two.reshape(TAPS, 16, C)


def solution(mesh):
    in_specs = (
        P("dp", "space", None, None, None),
        P(None, "dp", None),
        P(None, "dp", None),
        P("dp", "space", None, None, None),
    )
    out_specs = (
        P("dp", "space", None, None, None),
        P("dp", "space", None, None, None),
        P(None, "dp", None),
        P(None, "dp", None),
    )
    return jax.shard_map(shards, mesh=mesh, in_specs=in_specs, out_specs=out_specs, check_vma=False)
```

```python
import functools

import jax
import jax.numpy as jnp
from jax import lax
from jax.experimental import pallas as pl
from jax.experimental.pallas import tpu as pltpu
from jax.sharding import PartitionSpec as P

MESH = pl.DeviceIdType.MESH
F32 = jnp.float32
BF16 = jnp.bfloat16
C = 256
TAPS = 27
ROWS = TAPS * 16
TILES = 2 * TAPS
SHARE = -(-TILES // 8)


def dot(a, b, dims=((1,), (0,))):
    return lax.dot_general(a, b, (dims, ((), ())), preferred_element_type=F32)


def lanes():
    return lax.broadcasted_iota(jnp.int32, (16, 128), 1)


def lower(rows=16):
    return lax.broadcasted_iota(jnp.int32, (rows, 128), 1) < 64


def half_turn(v):
    return pltpu.roll(v, 64, 1)


def inside(j, k, sign):
    lane = lanes()
    y = (lane // 8) % 8 + sign * (j - 1)
    z = lane % 8 + sign * (k - 1)
    return (y >= 0) & (y < 8) & (z >= 0) & (z < 8)


def shifted(v, j, k, sign):
    delta = sign * (8 * (j - 1) + (k - 1))
    if delta == 0:
        return v
    parts = v.shape[0] // 16
    keep = inside(j, k, sign)
    if parts > 1:
        keep = jnp.concatenate([keep] * parts, axis=0)
    return jnp.where(keep, pltpu.roll(v, (-delta) % 128, 1), 0.0)


def regroup(w_ref, z_ref):
    group = lanes() // 16
    for q in range(4):
        for h in range(2):
            tiles = []
            for i in range(8):
                tap = 8 * q + i
                if tap < TAPS:
                    tiles.append(w_ref[16 * tap : 16 * tap + 16, 128 * h : 128 * h + 128].astype(F32))
                else:
                    tiles.append(jnp.zeros((16, 128), F32))
            for bit in (1, 2, 4):
                low = (group & bit) == 0
                for i in range(8):
                    if i & bit:
                        continue
                    a, b = tiles[i], tiles[i + bit]
                    tiles[i] = jnp.where(low, a, pltpu.roll(b, 16 * bit, 1))
                    tiles[i + bit] = jnp.where(low, pltpu.roll(a, 128 - 16 * bit, 1), b)
            for i in range(8):
                z_ref[8 * h + i, :, 128 * q : 128 * q + 128] = tiles[i].astype(BF16)


def gather_taps(y_ref, p_ref, hm_ref, hp_ref, sign):
    lo = lower()
    lefts = []
    for half in range(2):
        at = slice(128 * half, 128 * half + 128)
        total = None
        for j in range(3):
            for k in range(3):
                rows = [16 * (9 * i + 3 * j + k) for i in range(3)]
                first, mid, last = [y_ref[r : r + 16, at] for r in rows]
                if sign < 0:
                    first, last = last, first
                inner = jnp.where(lo, first, last)
                outer = jnp.where(lo, last, first)
                term = shifted(jnp.concatenate([mid, inner, outer], axis=0), j, k, sign)
                total = term if total is None else total + term
        p_ref[:, at] = total[:16] + half_turn(total[16:32])
        lefts.append(total[32:])
    hm_ref[...] = jnp.where(lo, lefts[0], half_turn(lefts[1])).astype(hm_ref.dtype)
    hp_ref[...] = jnp.where(lo, half_turn(lefts[0]), lefts[1]).astype(hp_ref.dtype)


def spread_halo(hp, hm, first, final):
    lo = lower(hp.shape[0])
    hp = jnp.where(first, 0.0, hp.astype(F32))
    hm = jnp.where(final, 0.0, hm.astype(F32))
    return [jnp.where(lo, hp, half_turn(hm)), jnp.where(lo, half_turn(hp), hm)]


def edge_planes(v):
    lo = lower(v.shape[0])
    a, b = v[:, :128], v[:, 128:]
    return jnp.where(lo, a, half_turn(b)), jnp.where(lo, half_turn(a), b)


def scatter_taps(v, halos, im_ref):
    lo = lower()
    for half in range(2):
        at = slice(128 * half, 128 * half + 128)
        own = v[:, at]
        turned = half_turn(own)
        stack = jnp.concatenate(
            [jnp.where(lo, halos[half], turned), own, jnp.where(lo, turned, halos[half])], axis=0
        )
        for j in range(3):
            for k in range(3):
                term = shifted(stack, j, k, 1).astype(BF16)
                for i in range(3):
                    row = 16 * (9 * i + 3 * j + k)
                    im_ref[row : row + 16, at] = term[16 * i : 16 * i + 16]


def kernel(
    factor,
    x_hbm, g_hbm, w1_hbm, w2_hbm,
    cells_hbm, grads_hbm,
    x_ref, g_ref, w1, w2,
    ga, gb, z1, z2, r1, r2, f1, f2, y_ref, p_ref, hm1, hp1, rhm1, rhp1, hm2, hp2, rhm2, rhp2,
    xm, xp, rxm, rxp, am, ap, ram, rap, imx, ima, gsum, gout, gin2, mine, sent, rr, part, other, full, oc, oall,
    in_sem, out_sem, w_send, w_recv, v_send, v_recv, a_send, a_recv,
    h_send, h_recv, n_send, n_recv, c_send, c_recv, r_send, r_recv, x_send, x_recv, f_send, f_recv, o_send, o_recv,
):
    d = lax.axis_index("dp")
    s = lax.axis_index("space")
    m, e = d // 2, d % 2
    xl, y = m // 4, m % 4
    z, xh = s // 2, s % 2
    above = lax.rem(s + 1, 16)
    below = lax.rem(s + 15, 16)
    first, final = s == 0, s == 15
    sibling = 2 * m + 1 - e
    across = 2 * z + 1 - xh
    up, down, far = [lax.rem(y + step, 4) for step in (1, 3, 2)]
    side = (1 - xl) * 4
    U, D, O, X = xl * 4 + up, xl * 4 + down, xl * 4 + far, side + y
    XU, XD, XO = side + up, side + down, side + far
    channels = pl.ds(pl.multiple_of(m * 32, 32), 32)

    def rows_of(index, count):
        return pl.ds(pl.multiple_of(index * count, count), count)

    def remote(src, dst, send, recv, dp, space):
        return pltpu.make_async_remote_copy(
            src_ref=src, dst_ref=dst, send_sem=send, recv_sem=recv, device_id=(dp, space), device_id_type=MESH
        )

    def each(count, body, start=0):
        def step(i, carry):
            body(i)
            return carry

        lax.fori_loop(start, count, step, 0)

    barrier = pltpu.get_barrier_semaphore()

    def greet(dp, space):
        pl.semaphore_signal(barrier, inc=1, device_id=(dp, space), device_id_type=MESH)

    each(8, lambda r: greet(2 * lax.rem(m + r, 8) + e, s), 1)
    each(8, lambda r: greet(d, 2 * lax.rem(z + r, 8) + xh), 1)
    greet(sibling, s)
    greet(d, above)
    greet(d, below)
    each(4, lambda r: greet(2 * (side + r) + e, across))

    pairs = [(x_hbm, x_ref), (g_hbm, g_ref), (w1_hbm, w1.at[e]), (w2_hbm, w2.at[e])]
    loads = [pltpu.make_async_copy(src, dst, in_sem.at[i]) for i, (src, dst) in enumerate(pairs)]
    for load in loads:
        load.start()

    def block(phase, t, chip):
        if phase == 0:
            return ga.at[chip // 2, t, :, pl.ds(pl.multiple_of(lax.rem(chip, 2) * 128, 128), 128)]
        return gb.at[t, :, rows_of(chip, 32), :]

    HOPS = [
        (m, None, X, X), (m, None, U, D), (m, None, D, U), (X, None, U, XD), (X, None, D, XU),
        (D, 0, U, O), (U, 1, D, O), (XD, 0, U, XO), (XU, 1, D, XO),
    ]

    def hop(phase, t, kind, arriving=False):
        chip, half, to, source = HOPS[kind]
        ref = block(phase, t, source if arriving else chip)
        if half is not None:
            ref = ref.at[pl.ds(128 * half, 128)] if phase == 0 else ref.at[pl.ds(2 * half, 2)]
        return remote(ref, ref, a_send.at[phase, t, kind], a_recv.at[phase, t, kind], 2 * to + e, s)

    def landed(phase, t, *kinds):
        for kind in kinds:
            hop(phase, t, kind, True).wait_recv()

    def depart(phase, t):
        for kind in range(3):
            hop(phase, t, kind).start()

    def relay(phase, t):
        for kind, then in ((0, (3, 4)), (1, (5,)), (2, (6,))):
            landed(phase, t, kind)
            for more in then:
                hop(phase, t, more).start()

    def relay_more(phase, t):
        for kind, more in ((3, 7), (4, 8)):
            landed(phase, t, kind)
            hop(phase, t, more).start()

    def slices(which, src, r, to, source):
        space = jnp.where(to // 4 == xl, s, across)
        return remote(
            src.at[pl.ds(2 * to, 2)], r.at[:, source, e],
            w_send.at[which, to], w_recv.at[which, source], 2 * to + e, space,
        )

    def cores(index, src, dst):
        return remote(src, dst, v_send.at[index], v_recv.at[index], sibling, s)

    def send_slices(which, src, r):
        each(8, lambda step: slices(which, src, r, lax.rem(m + step, 8), m).start(), 1)
        for slot in range(2):
            r[slot, m, e] = src[2 * m + slot]

    def pass_slices(which, src, r):
        def body(step):
            at = lax.rem(m + 8 - step, 8)
            slices(which, src, r, at, at).wait_recv()

        each(8, body, 1)
        cores(which, r.at[:, :, e], r.at[:, :, e]).start()

    def wait_slices(which, r, f):
        cores(which, r.at[:, :, 1 - e], r.at[:, :, 1 - e]).wait_recv()
        for slot in range(2):
            f[slot] = r[slot].reshape(C, 512).astype(F32).T.astype(BF16)

    mine_at = pl.ds(pl.multiple_of(lax.rem(m, 2) * 128, 128), 128)
    loads[0].wait()
    ga[m // 2, 0, :, mine_at] = x_ref[...].astype(F32).T.astype(BF16)
    loads[1].wait()
    ga[m // 2, 1, :, mine_at] = g_ref[...].astype(F32).T.astype(BF16)
    loads[2].wait()
    regroup(w1.at[e], z1)
    loads[3].wait()
    regroup(w2.at[e], z2)
    sent[:, TILES:] = jnp.zeros((2, 8 * SHARE - TILES, 16, 128), BF16)
    mine[:, TILES:] = jnp.zeros((2, 8 * SHARE - TILES, 16, 128), F32)
    pl.semaphore_wait(barrier, 21)

    depart(0, 0)
    send_slices(0, z1, r1)
    depart(0, 1)
    cores(2, w2.at[e], w2.at[e]).start()
    relay(0, 0)
    pass_slices(0, z1, r1)
    relay(0, 1)
    relay_more(0, 0)
    wait_slices(0, r1, f1)
    cores(2, w2.at[1 - e], w2.at[1 - e]).wait_recv()

    hm, hp, rhm, rhp = (hm1, hm2), (hp1, hp2), (rhm1, rhm2), (rhp1, rhp2)

    def halo_copies(phase, pair):
        return (
            remote(hm[phase].at[pair], rhm[phase].at[pair], h_send.at[phase, 0, pair], h_recv.at[phase, 0, pair], d, below),
            remote(hp[phase].at[pair], rhp[phase].at[pair], h_send.at[phase, 1, pair], h_recv.at[phase, 1, pair], d, above),
        )

    own_pair, other_pair = xl * 2 + y // 2, xl * 2 + 1 - y // 2
    ORDER = [own_pair, other_pair, side // 2 + y // 2, side // 2 + 1 - y // 2]

    def pair_at(i):
        pair = ORDER[0]
        for at in range(1, 4):
            pair = jnp.where(i == at, ORDER[at], pair)
        return pair

    def convolve(phase, pair, f, v, w, g):
        for slot in range(2):
            rows = pl.ds(16 * slot, 16)
            for t in range(2):
                y = y_ref.at[2 * slot + t]
                y[...] = dot(f[slot, :ROWS], v()) if t == 0 else dot(w[slot], g())
                gather_taps(
                    y, p_ref.at[t, pair, rows], hm[phase].at[pair, t, rows], hp[phase].at[pair, t, rows], 1 - 2 * t
                )
        for copy in halo_copies(phase, pair):
            copy.start()

    def phase_one(i):
        for at, kinds in ((1, (5, 6)), (3, (7, 8))):
            @pl.when(i == at)
            def _():
                if at == 1:
                    relay_more(0, 1)
                for t in range(2):
                    landed(0, t, *kinds)

        pair = pair_at(i)
        convolve(0, pair, f1, lambda: ga[pair, 0], w2, lambda: ga[pair, 1])

    each(4, phase_one)
    cores(3, w1.at[e], w1.at[e]).start()
    send_slices(1, z2, r2)

    def near(index, src, dst, to):
        return remote(src, dst, n_send.at[index], n_recv.at[index], d, to)

    def x_edges(pair):
        lowest, highest = edge_planes(ga[pair, 0, channels, :].astype(F32))
        xm[pair] = lowest.astype(BF16)
        xp[pair] = highest.astype(BF16)


    def halo_of(phase, t, pair):
        return jnp.concatenate(spread_halo(rhp[phase][pair, t], rhm[phase][pair, t], first, final), axis=1)

    def middle(i):
        pair = pair_at(i)
        for copy in halo_copies(0, pair):
            copy.wait_recv()
        pre = p_ref[0, pair] + halo_of(0, 0, pair)
        grad = p_ref[1, pair] + halo_of(0, 1, pair)
        sig = jax.nn.sigmoid(pre)
        act = (pre * sig).astype(BF16)
        gb[0, pair, channels, :] = act
        gb[1, pair, channels, :] = (grad * sig * (1.0 + pre * (1.0 - sig))).astype(BF16)

    each(4, middle)
    depart(1, 1)

    def act_edges(pair):
        lowest, highest = edge_planes(gb[0, pair, channels, :].astype(F32))
        am[pair] = lowest.astype(BF16)
        ap[pair] = highest.astype(BF16)

    each(4, act_edges)
    near(2, am, ram, below).start()
    near(3, ap, rap, above).start()
    depart(1, 0)
    each(4, x_edges)
    near(0, xm, rxm, below).start()
    near(1, xp, rxp, above).start()

    def taps(pair, v, up_halo, down_halo, im):
        for slot in range(2):
            rows = slice(16 * slot, 16 * slot + 16)
            halos = spread_halo(up_halo[pair, rows], down_halo[pair, rows], first, final)
            scatter_taps(v[rows], halos, im.at[pair, slot])

    def taps_x(pair):
        taps(pair, ga[pair, 0, channels, :].astype(F32), rxp, rxm, imx)

    def taps_a(pair):
        taps(pair, gb[0, pair, channels, :].astype(F32), rap, ram, ima)

    def core_copy(which):
        return remote(gout.at[which], gin2.at[which], c_send.at[which], c_recv.at[which], sibling, s)

    def reduce_copy(which, step):
        to = lax.rem(z + step, 8)
        return remote(
            sent.at[which, pl.ds(to * SHARE, SHARE)], rr.at[which, step],
            r_send.at[which, step], r_recv.at[which, step], d, 2 * to + xh,
        )

    def product(im, slot, operand, total):
        total[...] = dot(im[0, slot], operand(0), ((1,), (1,)))

        def add(pair):
            total[...] += dot(im[pair, slot], operand(pair), ((1,), (1,)))

        each(4, add, 1)

    def send_partial(which, im, operand):
        product(im, 1 - e, operand, gout.at[which])
        core_copy(which).start()
        product(im, e, operand, gsum)
        core_copy(which).wait_recv()
        for tile in range(TILES):
            row, lane = tile // 2 * 16, tile % 2 * 128
            at = (slice(row, row + 16), slice(lane, lane + 128))
            value = gsum[at] + gin2[(which, *at)]
            mine[which, tile] = value
            sent[which, tile] = value.astype(BF16)
        for step in (4, 3, 5, 2, 6, 1, 7):
            reduce_copy(which, step).start()

    def pair_copy(which):
        return remote(part.at[which], other.at[which], x_send.at[which], x_recv.at[which], d, 2 * z + 1 - xh)

    def reduce_ring(which):
        each(8, lambda step: reduce_copy(which, step).wait_recv(), 1)
        total = mine[which, pl.ds(z * SHARE, SHARE)]
        for step in range(1, 8):
            total += rr[which, step].astype(F32)
        part[which] = total
        pair_copy(which).start()

    CUT = SHARE // 2 + 1
    STEPS = [
        (0, 0, SHARE, 2), (0, 0, SHARE, -2),
        (-2, 0, SHARE, -1), (-2, 0, SHARE, 1), (2, 0, SHARE, 1), (2, 0, SHARE, -1),
        (-2, 0, CUT, 2), (2, CUT, SHARE, -2),
    ]

    def spread_copy(which, kind, arriving=False):
        owner, low, high, far_to = STEPS[kind]
        if arriving:
            owner = owner - far_to
        ref = full.at[which, pl.ds(lax.rem(z + owner + 8, 8) * SHARE + low, high - low)]
        to = 2 * lax.rem(z + far_to + 8, 8) + xh
        return remote(ref, ref, f_send.at[which, kind], f_recv.at[which, kind], d, to)

    def spread(which):
        pair_copy(which).wait_recv()
        full[which, pl.ds(z * SHARE, SHARE)] = ((part[which] + other[which]) * factor).astype(BF16)
        spread_copy(which, 0).start()
        spread_copy(which, 1).start()

    def spread_on(which):
        for kind, then in ((0, (6, 3, 2)), (1, (7, 5, 4))):
            spread_copy(which, kind, True).wait_recv()
            for more in then:
                spread_copy(which, more).start()

    def result(which):
        src, dst = (oall, cells_hbm) if which == 2 else (full.at[which], grads_hbm.at[which])
        return pltpu.make_async_copy(src, dst, out_sem.at[which])

    def spread_end(which):
        for kind in range(2, 8):
            spread_copy(which, kind, True).wait_recv()
        result(which).start()

    relay(1, 1)
    near(2, am, ram, below).wait_recv()
    near(3, ap, rap, above).wait_recv()
    each(4, taps_a)
    relay(1, 0)
    relay_more(1, 1)
    send_partial(1, ima, lambda pair: ga[pair, 1])
    near(0, xm, rxm, below).wait_recv()
    near(1, xp, rxp, above).wait_recv()
    each(4, taps_x)
    relay_more(1, 0)
    landed(1, 1, 5, 6, 7, 8)
    send_partial(0, imx, lambda pair: gb[1, pair])
    pass_slices(1, z2, r2)
    landed(1, 0, 5, 6, 7, 8)
    wait_slices(1, r2, f2)
    cores(3, w1.at[1 - e], w1.at[1 - e]).wait_recv()

    def phase_two(i):
        @pl.when(i == 2)
        def _():
            reduce_ring(1)

        pair = pair_at(i)
        convolve(1, pair, f2, lambda: gb[0, pair], w1, lambda: gb[1, pair])

    each(4, phase_two)
    reduce_ring(0)
    spread(1)

    def home(to, source):
        return remote(oc.at[to], oall.at[source], o_send.at[to], o_recv.at[source], 2 * to + e, s)

    def finish(i):
        pair = pair_at(i)
        for copy in halo_copies(1, pair):
            copy.wait_recv()
        for t in range(2):
            total = p_ref[t, pair] + halo_of(1, t, pair)
            total = (ga[pair, t, channels, :].astype(F32) + total).astype(BF16)
            oc[2 * pair, t] = total[:, :128]
            oc[2 * pair + 1, t] = total[:, 128:]
        for half in range(2):
            to = 2 * pair + half

            @pl.when(to != m)
            def _():
                home(to, m).start()

    each(4, finish)
    spread(0)
    spread_on(1)
    oall[m] = oc[m]

    def wait_home(step):
        source = lax.rem(m + 8 - step, 8)
        home(source, source).wait_recv()

    each(8, wait_home, 1)
    result(2).start()
    spread_on(0)
    spread_end(1)
    spread_end(0)
    for which in range(3):
        result(which).wait()

    def wait_far(step):
        to = lax.rem(m + step, 8)
        home(to, m).wait_send()
        slices(0, z1, r1, to, m).wait_send()
        slices(1, z2, r2, to, m).wait_send()
        for which in range(2):
            reduce_copy(which, step).wait_send()

    each(8, wait_far, 1)

    def wait_halo(pair):
        for phase in range(2):
            for copy in halo_copies(phase, pair):
                copy.wait_send()

    each(4, wait_halo)
    cores(0, r1.at[:, :, e], r1.at[:, :, e]).wait_send()
    cores(1, r2.at[:, :, e], r2.at[:, :, e]).wait_send()
    cores(2, w2.at[e], w2.at[e]).wait_send()
    cores(3, w1.at[e], w1.at[e]).wait_send()
    for t in range(2):
        core_copy(t).wait_send()
        pair_copy(t).wait_send()
        for kind in range(8):
            spread_copy(t, kind).wait_send()
        for phase in range(2):
            for kind in range(9):
                hop(phase, t, kind).wait_send()
    near(0, xm, rxm, below).wait_send()
    near(1, xp, rxp, above).wait_send()
    near(2, am, ram, below).wait_send()
    near(3, ap, rap, above).wait_send()


def lay_out(cells_ref, grads_ref, out_ref, gin_ref, one_ref, two_ref):
    for t, ref in enumerate((out_ref, gin_ref)):
        ref[...] = cells_ref[:, t].reshape(C, 128).astype(F32).T.astype(BF16)
    for which, ref in enumerate((one_ref, two_ref)):
        for tile in range(TILES):
            row, lane = tile // 2 * 16, tile % 2 * 128
            ref[row : row + 16, lane : lane + 128] = grads_ref[which, tile].astype(F32)


def shards(features, weight_one, weight_two, cotangent):
    shape = features.shape
    count = shape[0] * lax.axis_size("dp") * shape[1] * lax.axis_size("space") * shape[2] * shape[3]
    factor = float(count) ** (-0.5)
    vmem = pl.BlockSpec(memory_space=pltpu.VMEM)
    dma = pltpu.SemaphoreType.DMA
    scratch = pltpu.VMEM
    cells, grads = pl.pallas_call(
        functools.partial(kernel, factor),
        out_shape=[
            jax.ShapeDtypeStruct((8, 2, 32, 128), BF16),
            jax.ShapeDtypeStruct((2, 8 * SHARE, 16, 128), BF16),
        ],
        in_specs=[pl.BlockSpec(memory_space=pl.ANY)] * 4,
        out_specs=[pl.BlockSpec(memory_space=pl.ANY)] * 2,
        scratch_shapes=[
            scratch((128, C), BF16), scratch((128, C), BF16),
            scratch((2, ROWS, C), BF16), scratch((2, ROWS, C), BF16),
            scratch((4, 2, C, C), BF16),
            scratch((2, 4, C, C), BF16),
            scratch((16, 16, 512), BF16), scratch((16, 16, 512), BF16),
            scratch((2, 8, 2, 16, 512), BF16), scratch((2, 8, 2, 16, 512), BF16),
            scratch((2, 512, C), BF16), scratch((2, 512, C), BF16),
            scratch((4, ROWS, C), F32),
            scratch((2, 4, 32, C), F32),
            *[scratch((4, 2, 32, 128), F32)] * 4,
            *[scratch((4, 2, 32, 128), BF16)] * 4,
            *[scratch((4, 32, 128), BF16)] * 8,
            scratch((4, 2, ROWS, C), BF16), scratch((4, 2, ROWS, C), BF16),
            scratch((ROWS, C), F32),
            scratch((2, ROWS, C), F32), scratch((2, ROWS, C), F32),
            scratch((2, 8 * SHARE, 16, 128), F32),
            scratch((2, 8 * SHARE, 16, 128), BF16),
            scratch((2, 8, SHARE, 16, 128), BF16),
            scratch((2, SHARE, 16, 128), F32), scratch((2, SHARE, 16, 128), F32),
            scratch((2, 8 * SHARE, 16, 128), BF16),
            scratch((8, 2, 32, 128), BF16), scratch((8, 2, 32, 128), BF16),
            dma((4,)), dma((3,)),
            dma((2, 8)), dma((2, 8)), dma((4,)), dma((4,)),
            dma((2, 2, 9)), dma((2, 2, 9)),
            dma((2, 2, 4)), dma((2, 2, 4)),
            dma((4,)), dma((4,)), dma((2,)), dma((2,)),
            dma((2, 8)), dma((2, 8)), dma((2,)), dma((2,)), dma((2, 8)), dma((2, 8)),
            dma((8,)), dma((8,)),
        ],
        compiler_params=pltpu.CompilerParams(
            collective_id=0, has_side_effects=True, vmem_limit_bytes=56 * 2**20
        ),
    )(
        features.reshape(128, C), cotangent.reshape(128, C),
        weight_one.reshape(ROWS, C), weight_two.reshape(ROWS, C),
    )
    out, gin, one, two = pl.pallas_call(
        lay_out,
        out_shape=[
            jax.ShapeDtypeStruct((128, C), BF16),
            jax.ShapeDtypeStruct((128, C), BF16),
            jax.ShapeDtypeStruct((ROWS, C), F32),
            jax.ShapeDtypeStruct((ROWS, C), F32),
        ],
        in_specs=[vmem] * 2,
        out_specs=[vmem] * 4,
    )(cells, grads)
    return out.reshape(shape), gin.reshape(shape), one.reshape(TAPS, 16, C), two.reshape(TAPS, 16, C)


def solution(mesh):
    in_specs = (
        P("dp", "space", None, None, None),
        P(None, "dp", None),
        P(None, "dp", None),
        P("dp", "space", None, None, None),
    )
    out_specs = (
        P("dp", "space", None, None, None),
        P("dp", "space", None, None, None),
        P(None, "dp", None),
        P(None, "dp", None),
    )
    return jax.shard_map(shards, mesh=mesh, in_specs=in_specs, out_specs=out_specs, check_vma=False)
```
